32 devices in a mesh: seq: 8 (over z, y), clip: 4 (over x, core).
Axes of the slice: x: 2, y: 2, z: 4, core: 2. Of those that a mesh axis runs over, the one named last changes fastest.
Arguments:
- tokens: bfloat16 [12288, 1536], P(('clip', 'seq')), parts along dimension 0, may hold values from -16 to 16
- w_qkv: bfloat16 [1536, 2304], P('seq'), may hold values from -0.15625 to 0.15625
- w_out: bfloat16 [768, 1536], P(None, 'seq'), may hold values from -0.21875 to 0.21875
- key_blocks: int32 [192, 4], P(('clip', 'seq')), parts along dimension 0, may hold values from 0 to 47, as said below
- key_levels: int32 [192, 4], P(('clip', 'seq')), parts along dimension 0, may hold values from 1 to 2
Outputs:
- mixed: bfloat16 [12288, 1536], P(('clip', 'seq')), parts along dimension 0
The draws below stay inside these ranges and needn't reach their ends.
There are 4 independent parts, one for each index of `clip`. The reference program is written for one: setup_inputs(seed, part) draws one part's arguments, and reference() takes and returns one part's arrays. A program takes and returns all parts, laid end to end along the dimension named above; an argument that names none is the same for every part. Nothing has to cross between parts.
Inputs may be any that keep to these rules, and one draw needn't show every extreme that they name: `key_blocks`: among the 24 entries of the query blocks of one device (aligned rows of 6), the blocks of any one device (block // 6) are named at most 3 times, and in every draw the blocks of some device exactly 3 times.
All inputs are finite; a program needn't handle non-finite values.
Results may differ from the reference program's by a relative error of at most 0.012.
The reference program's roundings to bfloat16 on the way count: a program that leaves them out, or rounds other values in their place, can miss the bound.
Values may be sent and summed in bfloat16 or wider, within the bound.
A program may use at most 128 MiB of HBM per device.

```python
import math
import jax
import jax.numpy as jnp
from jax import lax

D = 1536
HEADS = 6
HD = 128
BLK = 64
QUART = 16
BLK_DEV = 6
HW = 768
TOKENS = 3072
NB = 48
LIST = 4
SLOTS = 3


def draw_tokens(key, part):
    key = jax.random.fold_in(key, 7)
    base_key = jax.random.fold_in(key, 0)
    values = jax.random.normal(base_key, (TOKENS, D), jnp.float32)
    return jnp.clip(values, -6.0, 6.0).astype(jnp.bfloat16)


def draw_key_blocks(key, part):
    key = jax.random.fold_in(key, 19)
    devices = NB // BLK_DEV
    entries = BLK_DEV * LIST
    pair_count = devices * SLOTS

    def one_device(device_index):
        device_key = jax.random.fold_in(key, device_index)
        order_key, chosen_key, shuffle_key, local_key = jax.random.split(device_key, 4)
        inverse = jnp.argsort(jax.random.permutation(order_key, pair_count)).astype(jnp.int32)
        owner_of = jnp.arange(pair_count, dtype=jnp.int32) % devices
        chosen = jax.random.randint(chosen_key, (), 0, devices)
        priority = jnp.where(owner_of == chosen, 0, pair_count) + inverse
        picked = jnp.argsort(priority)[:entries]
        owner_ids = owner_of[picked][jax.random.permutation(shuffle_key, entries)]
        local_ids = jax.random.randint(local_key, (entries,), 0, BLK_DEV)
        return (owner_ids * BLK_DEV + local_ids).reshape(BLK_DEV, LIST)
    return jax.vmap(one_device)(jnp.arange(devices, dtype=jnp.int32)).reshape(NB, LIST).astype(jnp.int32)


def draw_key_levels(key, part):
    key = jax.random.fold_in(key, 23)
    devices = NB // BLK_DEV
    share_key, dice_key = jax.random.split(key)
    level_share = jax.random.randint(share_key, (devices, 1, 1), 5, 96)
    dice_roll = jax.random.randint(dice_key, (devices, BLK_DEV, LIST), 0, 100)
    return jnp.where(dice_roll < level_share, 1, 2).astype(jnp.int32).reshape(NB, LIST)


def level_of(rng, dims, cuts, low, high):
    def one(axis_at, shards_of):
        heights = jax.random.uniform(jax.random.fold_in(jax.random.fold_in(rng, 6), axis_at), (shards_of,), jnp.float32, low / len(cuts), high / len(cuts))
        return jnp.repeat(jnp.exp(heights), dims[axis_at] // shards_of).reshape((-1,) + (1,) * (len(dims) - axis_at - 1))

    level = one(*cuts[0])
    for cut in cuts[1:]:
        level = level * one(*cut)
    return level


def normal_values(rng, shape, width, limit, pieces=(), kind=jnp.bfloat16):
    values = width * jax.random.normal(rng, shape, jnp.float32)
    if pieces:
        values = values * level_of(rng, shape, pieces, -0.22, 0.18)
    return jnp.clip(values, -limit, limit).astype(kind)


def setup_inputs(seed: int = 0, part: int = 0) -> dict:
    key_of = jax.random.split(jax.random.key(seed), 6)
    part_keys = jax.random.split(jax.random.fold_in(key_of[5], part), 6)
    tokens = draw_tokens(jax.random.fold_in(jax.random.fold_in(key_of[5], part), 71), part)
    w_qkv = normal_values(key_of[1], (D, 3 * HW), D ** -0.5, 0.15625, ((0, 8),))
    w_out = normal_values(key_of[2], (HW, D), HW ** -0.5, 0.21875, ((1, 8),))
    key_blocks = draw_key_blocks(jax.random.fold_in(jax.random.fold_in(key_of[5], part), 71), part)
    key_levels = draw_key_levels(jax.random.fold_in(jax.random.fold_in(key_of[5], part), 71), part)
    return dict(tokens=tokens, w_qkv=w_qkv, w_out=w_out, key_blocks=key_blocks, key_levels=key_levels)


masked_score = -1e+30

def attend_one(queries, keys_all, score_bias, usable):
    heads_view = keys_all.reshape(keys_all.shape[0], 2, HEADS, HD).astype(jnp.float32)
    scores = jnp.einsum('qhd,khd->hqk', queries.astype(jnp.float32), heads_view[:, 0])
    scores = scores * (1.0 / math.sqrt(HD)) + score_bias
    scores = jnp.where(usable, scores, masked_score)
    row_top = lax.optimization_barrier(jnp.max(scores, axis=-1, keepdims=True))
    exponent = jnp.exp(scores - row_top)
    total_mass = lax.optimization_barrier(jnp.sum(exponent, axis=-1, keepdims=True))
    attn_weights = (exponent / total_mass).astype(jnp.bfloat16)
    attended = jnp.einsum('hqk,khd->qhd', attn_weights.astype(jnp.float32), heads_view[:, 1])
    return attended.astype(jnp.bfloat16)

def reference(tokens, w_qkv, w_out, key_blocks, key_levels):
    head_width = HEADS * HD
    projected = jnp.dot(tokens, w_qkv, preferred_element_type=jnp.float32).astype(jnp.bfloat16)
    queries = projected[:, :head_width].reshape(NB, BLK, HEADS, HD)
    kv_blocks = projected[:, head_width:].reshape(NB, BLK, 2 * head_width)
    widened = kv_blocks.astype(jnp.float32).reshape(NB, QUART, BLK // QUART, 2 * head_width)
    coarse_all = lax.optimization_barrier(jnp.mean(widened, axis=2)).astype(jnp.bfloat16)
    list_len = key_blocks.shape[1]
    offsets = jnp.arange(3, dtype=jnp.int32) - 1
    score_bias = jnp.concatenate([jnp.zeros((3 * BLK,), jnp.float32), jnp.full((list_len * QUART,), math.log(BLK / QUART), jnp.float32), jnp.full((list_len,), math.log(BLK), jnp.float32)])

    def one_block(block_index):
        near_ids = block_index + offsets
        near_ok = (near_ids >= 0) & (near_ids < NB)
        near_rows = kv_blocks[jnp.clip(near_ids, 0, NB - 1)].reshape(3 * BLK, 2 * head_width)
        named_ids = key_blocks[block_index]
        level_ids = key_levels[block_index]
        coarse_rows = coarse_all[named_ids]
        single_rows = lax.optimization_barrier(jnp.mean(coarse_rows.astype(jnp.float32), axis=1)).astype(jnp.bfloat16)
        keys_all = jnp.concatenate([near_rows, coarse_rows.reshape(list_len * QUART, 2 * head_width), single_rows], axis=0)
        usable = jnp.concatenate([jnp.repeat(near_ok, BLK), jnp.repeat(level_ids == 1, QUART), level_ids == 2])
        return attend_one(queries[block_index], keys_all, score_bias, usable).reshape(BLK, head_width)
    attended = lax.map(one_block, jnp.arange(NB, dtype=jnp.int32)).reshape(TOKENS, head_width)
    return jnp.dot(attended, w_out, preferred_element_type=jnp.float32).astype(jnp.bfloat16)
```

```python
import functools
import math

import jax
import jax.numpy as jnp
from jax import lax
from jax.experimental import pallas as pl
from jax.experimental.pallas import tpu as pltpu
from jax.sharding import PartitionSpec as P

HEADS = 6
HD = 128
BLK = 64
QUART = 16


masked_score = -1e30


def with_halo(block, sides, width):
    for axis, dim in sides:
        count = lax.axis_size(axis)
        forward = [(i, i + 1) for i in range(count - 1)]
        backward = [(target, source) for source, target in forward]
        low = lax.ppermute(
            lax.slice_in_dim(block, block.shape[dim] - width, None, axis=dim), axis, forward
        )
        high = lax.ppermute(lax.slice_in_dim(block, 0, width, axis=dim), axis, backward)
        block = jnp.concatenate([low, block, high], axis=dim)
    return block


def attend(queries, keys_all, score_bias, usable):
    block_count, key_count = (keys_all.shape[0], keys_all.shape[1])
    heads_view = keys_all.reshape(block_count, key_count, 2, HEADS, HD)
    scores = jnp.einsum(
        "bqhd,bkhd->bhqk", queries, heads_view[:, :, 0], preferred_element_type=jnp.float32
    )
    scores = scores * (1.0 / math.sqrt(HD)) + score_bias[:, None, None, :]
    scores = jnp.where(usable[:, None, None, :], scores, masked_score)
    row_top = jnp.max(scores, axis=-1, keepdims=True)
    exponent = jnp.exp(scores - row_top)
    total_mass = jnp.sum(exponent, axis=-1, keepdims=True)
    attn_weights = (exponent / total_mass).astype(jnp.bfloat16)
    attended = jnp.einsum(
        "bhqk,bkhd->bqhd", attn_weights, heads_view[:, :, 1], preferred_element_type=jnp.float32
    )
    return attended.astype(jnp.bfloat16)


def per_device_general(tokens, w_qkv, w_out, key_blocks, key_levels):
    peer_count = lax.axis_size("seq")
    own_index = lax.axis_index("seq")
    tok_rows = tokens.shape[0]
    local_blocks = tok_rows // BLK
    list_len = key_blocks.shape[1]
    slot_count = (local_blocks * list_len + peer_count - 1) // peer_count
    head_width = HEADS * HD
    projected = jnp.dot(
        tokens, lax.all_gather(w_qkv, "seq", axis=0, tiled=True), preferred_element_type=jnp.float32
    ).astype(jnp.bfloat16)
    queries = projected[:, :head_width]
    key_value = projected[:, head_width:]
    kv_blocks = key_value.reshape(local_blocks, BLK, 2 * head_width)
    widened = kv_blocks.astype(jnp.float32).reshape(
        local_blocks, QUART, BLK // QUART, 2 * head_width
    )
    coarse_own = jnp.mean(widened, axis=2).astype(jnp.bfloat16)
    flat_ids = key_blocks.reshape(-1)
    owner_ids = flat_ids // local_blocks
    local_ids = flat_ids % local_blocks
    peer_ids = jnp.arange(peer_count, dtype=jnp.int32)
    slot_ids = jnp.arange(slot_count, dtype=jnp.int32)
    owner_hot = (owner_ids[:, None] == peer_ids[None, :]).astype(jnp.int32)
    slot_rank = jnp.sum((jnp.cumsum(owner_hot, axis=0) - owner_hot) * owner_hot, axis=1)
    slot_hot = (slot_rank[:, None] == slot_ids[None, :]).astype(jnp.int32)
    wanted = jnp.sum(
        owner_hot[:, :, None] * slot_hot[:, None, :] * local_ids[:, None, None], axis=0
    )
    received = lax.all_to_all(
        coarse_own[lax.all_to_all(wanted, "seq", split_axis=0, concat_axis=0, tiled=True)],
        "seq",
        split_axis=0,
        concat_axis=0,
        tiled=True,
    )
    coarse_rows = received[owner_ids, slot_rank]
    single_rows = jnp.mean(coarse_rows.astype(jnp.float32), axis=1).astype(jnp.bfloat16)
    padded = with_halo(kv_blocks, (("seq", 0),), 1)
    near_rows = jnp.concatenate([padded[:-2], padded[1:-1], padded[2:]], axis=1)
    near_ids = (
        own_index * local_blocks
        + jnp.arange(local_blocks, dtype=jnp.int32)[:, None]
        + jnp.arange(3, dtype=jnp.int32)[None, :]
        - 1
    )
    near_ok = (near_ids >= 0) & (near_ids < local_blocks * peer_count)
    keys_all = jnp.concatenate(
        [
            near_rows,
            coarse_rows.reshape(local_blocks, list_len * QUART, 2 * head_width),
            single_rows.reshape(local_blocks, list_len, 2 * head_width),
        ],
        axis=1,
    )
    usable = jnp.concatenate(
        [
            jnp.repeat(near_ok, BLK, axis=1),
            jnp.repeat(key_levels == 1, QUART, axis=1),
            key_levels == 2,
        ],
        axis=1,
    )
    score_bias = jnp.concatenate(
        [
            jnp.zeros((local_blocks, 3 * BLK), jnp.float32),
            jnp.full((local_blocks, list_len * QUART), math.log(BLK / QUART), jnp.float32),
            jnp.full((local_blocks, list_len), math.log(BLK), jnp.float32),
        ],
        axis=1,
    )
    attended = attend(queries.reshape(local_blocks, BLK, HEADS, HD), keys_all, score_bias, usable)
    attended = attended.reshape(tok_rows, head_width)
    return jnp.dot(
        attended,
        lax.all_gather(w_out, "seq", axis=1, tiled=True),
        preferred_element_type=jnp.float32,
    ).astype(jnp.bfloat16)


MESH = pl.DeviceIdType.MESH
LANES = 128


def fused_kernel(
    n, blocks, list_len,
    blocks_ref, levels_ref, tok_ref, w_ref, wo_ref, out_ref,
    w_all, wo_all, c_all, rows_all, q_all, kv_all, single_all, att_all,
    ring_send, ring_recv, core_send, core_recv, x_send, x_recv, relay_send, relay_recv,
    c_send, c_recv, halo_send, halo_recv,
):
    me = lax.axis_index("seq")
    clip = lax.axis_index("clip")
    half = n // 2
    own = blocks * BLK
    listed = blocks * list_len * QUART
    near = own + 2 * BLK
    width = HEADS * HD

    def owner_at(pos):
        pos = lax.rem(pos + 2 * n, n)
        return jnp.where(pos < half, 2 * pos, 2 * (n - 1 - pos) + 1)

    pos = jnp.where(lax.rem(me, 2) == 0, me // 2, n - 1 - me // 2)
    ring = ((owner_at(pos + 1), clip), (owner_at(pos - 1), clip))
    core_q = clip + 1 - 2 * lax.rem(clip, 2)
    x_q = lax.rem(clip + 2, 4)
    core_peer, x_peer = (me, core_q), (me, x_q)
    after, before = (lax.rem(me + 1, n), clip), (lax.rem(me + n - 1, n), clip)

    barrier = pltpu.get_barrier_semaphore()
    for peer in (*ring, core_peer, x_peer, after, before):
        pl.semaphore_signal(barrier, inc=1, device_id=peer, device_id_type=MESH)
    pl.semaphore_wait(barrier, 6)

    def remote(src, dst, send, recv, peer):
        return pltpu.make_async_remote_copy(
            src_ref=src, dst_ref=dst, send_sem=send, recv_sem=recv,
            device_id=peer, device_id_type=MESH,
        )

    started = []

    def start(copy):
        copy.start()
        started.append(copy)

    shards = ((w_ref, w_all), (wo_ref, wo_all))

    def part(ref, slot, t, way):
        lanes = ref.shape[-1]
        if t < half:
            return ref.at[slot]
        return ref.at[slot, :, pl.ds(way * (lanes // 2), lanes // 2)]

    def owner_from(t, way):
        return owner_at(pos - t) if way == 0 else owner_at(pos + t)

    def ring_send_step(kind, t):
        for way in range(2):
            source, full = shards[kind]
            owner = owner_from(t - 1, way)
            slot = owner * 4 + clip
            src = part(source, clip, t, way) if t == 1 else part(full, slot, t, way)
            start(remote(
                src, part(full, slot, t, way),
                ring_send.at[kind, t - 1, way], ring_recv.at[kind, t - 1, way], ring[way],
            ))

    def arrive(kind, t, way):
        full = shards[kind][1]
        mine = part(full, owner_from(t, way) * 4 + clip, t, way)
        remote(
            mine, mine, ring_send.at[kind, t - 1, way], ring_recv.at[kind, t - 1, way], ring[way]
        ).wait_recv()

    def share(kind, t):
        full = shards[kind][1]
        for way in range(2):
            mine = part(full, owner_from(t, way) * 4 + clip, t, way)
            at = (kind, t - 1, way)
            start(remote(mine, mine, x_send.at[at], x_recv.at[at], x_peer))
            start(remote(mine, mine, core_send.at[at], core_recv.at[at], core_peer))

    def ring_step(kind, t):
        for way in range(2):
            arrive(kind, t, way)
        if t < half:
            ring_send_step(kind, t + 1)
        share(kind, t)

    def relay_step(kind, t):
        full = shards[kind][1]
        for way in range(2):
            at = (kind, t - 1, way)
            theirs = part(full, owner_from(t, way) * 4 + x_q, t, way)
            remote(theirs, theirs, x_send.at[at], x_recv.at[at], x_peer).wait_recv()
            start(remote(theirs, theirs, relay_send.at[at], relay_recv.at[at], core_peer))

    def finish_step(kind, t):
        full = shards[kind][1]
        for way in range(2):
            at = (kind, t - 1, way)
            owner = owner_from(t, way)
            one = part(full, owner * 4 + core_q, t, way)
            remote(one, one, core_send.at[at], core_recv.at[at], core_peer).wait_recv()
            two = part(full, owner * 4 + lax.rem(core_q + 2, 4), t, way)
            remote(two, two, relay_send.at[at], relay_recv.at[at], core_peer).wait_recv()

    def c_part(owner, t, way):
        if t < half:
            return c_all.at[pl.ds(owner * blocks, blocks)]
        return c_all.at[pl.ds(owner * blocks + way * (blocks // 2), blocks // 2)]

    def c_send_step(t):
        for way in range(2):
            piece = c_part(owner_from(t - 1, way), t, way)
            start(remote(
                piece, piece, c_send.at[t - 1, way], c_recv.at[t - 1, way], ring[way]
            ))

    def c_step(t):
        for way in range(2):
            piece = c_part(owner_from(t, way), t, way)
            remote(
                piece, piece, c_send.at[t - 1, way], c_recv.at[t - 1, way], ring[way]
            ).wait_recv()
        if t < half:
            c_send_step(t + 1)

    ring_send_step(0, 1)
    start(remote(
        tok_ref.at[pl.ds(own - BLK, BLK)], rows_all.at[pl.ds(0, BLK)],
        halo_send.at[0], halo_recv.at[0], after,
    ))
    start(remote(
        tok_ref.at[pl.ds(0, BLK)], rows_all.at[pl.ds(BLK + own, BLK)],
        halo_send.at[1], halo_recv.at[1], before,
    ))
    coarse_count = blocks * QUART
    fold = BLK // QUART
    to_row = lax.broadcasted_iota(jnp.int32, (coarse_count, own), 0)
    from_row = lax.broadcasted_iota(jnp.int32, (coarse_count, own), 1)
    mean_of = jnp.where(
        (from_row >= to_row * fold) & (from_row < (to_row + 1) * fold), 1.0 / fold, 0.0
    ).astype(jnp.bfloat16)
    means = jnp.dot(mean_of, tok_ref[...], preferred_element_type=jnp.float32)
    c_all[pl.ds(me * blocks, blocks)] = means.astype(jnp.bfloat16).reshape(
        blocks, QUART, tok_ref.shape[1]
    )
    c_send_step(1)
    w_all[pl.ds(me * 4, 4)] = w_ref[...]
    wo_all[pl.ds(me * 4, 4)] = wo_ref[...]
    rows_all[pl.ds(BLK, own), :] = tok_ref[...]

    for t in range(1, half + 1):
        ring_step(0, t)
        if t > 1:
            relay_step(0, t - 1)
        c_step(t)
    ring_send_step(1, 1)
    relay_step(0, half)
    for t in range(1, half + 1):
        finish_step(0, t)
    for low, high, side, peer in ((0, BLK, 0, after), (BLK + own, near, 1, before)):
        piece = rows_all.at[pl.ds(low, BLK)]
        remote(piece, piece, halo_send.at[side], halo_recv.at[side], peer).wait_recv()

    for b in range(blocks):
        for i in range(list_len):
            at = near + (b * list_len + i) * QUART
            rows_all[pl.ds(at, QUART), :] = c_all[blocks_ref[b, i]]

    depth = w_all.shape[0] * w_all.shape[1]
    tile = 256

    def q_tile(j, carry):
        columns = pl.ds(pl.multiple_of(j * tile, tile), tile)
        q_all[:, columns] = jnp.dot(
            rows_all[pl.ds(BLK, own), :], w_all[:, :, columns].reshape(depth, tile),
            preferred_element_type=jnp.float32,
        ).astype(jnp.bfloat16)
        return carry

    def kv_tile(j, carry):
        columns = pl.ds(pl.multiple_of(j * tile, tile), tile)
        there = pl.ds(pl.multiple_of(width + j * tile, tile), tile)
        kv_all[:, columns] = jnp.dot(
            rows_all[...], w_all[:, :, there].reshape(depth, tile),
            preferred_element_type=jnp.float32,
        ).astype(jnp.bfloat16)
        return carry

    lax.fori_loop(0, width // tile, q_tile, 0)
    ring_step(1, 1)
    lax.fori_loop(0, width // tile, kv_tile, 0)
    ring_step(1, 2)
    relay_step(1, 1)
    lax.fori_loop(width // tile, 2 * width // tile, kv_tile, 0)
    for t in range(3, half + 1):
        ring_step(1, t)
        relay_step(1, t - 1)

    to_row = lax.broadcasted_iota(jnp.int32, (LANES, listed), 0)
    from_row = lax.broadcasted_iota(jnp.int32, (LANES, listed), 1)
    one_of = jnp.where(
        (from_row >= to_row * QUART) & (from_row < (to_row + 1) * QUART), 1.0 / QUART, 0.0
    ).astype(jnp.bfloat16)
    single_all[...] = jnp.dot(
        one_of, kv_all[pl.ds(near, listed), :], preferred_element_type=jnp.float32
    ).astype(jnp.bfloat16)

    per = list_len * QUART
    key_count = 3 * BLK + per + LANES
    lane = lax.broadcasted_iota(jnp.int32, (1, key_count), 1)

    def attend_block(b, carry):
        bias = jnp.where(lane < 3 * BLK, 0.0, masked_score)
        bias = jnp.where((lane < BLK) & (me * blocks + b == 0), masked_score, bias)
        bias = jnp.where(
            (lane >= 2 * BLK) & (lane < 3 * BLK) & (me * blocks + b == n * blocks - 1),
            masked_score, bias,
        )
        for i in range(list_len):
            level = levels_ref[b, i]
            low = 3 * BLK + i * QUART
            bias = jnp.where(
                (lane >= low) & (lane < low + QUART) & (level == 1), math.log(BLK / QUART), bias
            )
            bias = jnp.where(
                (lane == 3 * BLK + per + b * list_len + i) & (level == 2), math.log(BLK), bias
            )
        q_rows = pl.ds(pl.multiple_of(b * BLK, BLK), BLK)
        near_rows = pl.ds(pl.multiple_of(b * BLK, BLK), 3 * BLK)
        far_rows = pl.ds(pl.multiple_of(near + b * per, per), per)
        for h in range(HEADS):
            k_lanes = pl.ds(h * HD, HD)
            v_lanes = pl.ds(width + h * HD, HD)
            keys = jnp.concatenate(
                [kv_all[near_rows, k_lanes], kv_all[far_rows, k_lanes], single_all[:, k_lanes]], 0
            )
            values = jnp.concatenate(
                [kv_all[near_rows, v_lanes], kv_all[far_rows, v_lanes], single_all[:, v_lanes]], 0
            )
            scores = lax.dot_general(
                q_all[q_rows, k_lanes], keys, (((1,), (1,)), ((), ())),
                preferred_element_type=jnp.float32,
            )
            scores = scores * (1.0 / math.sqrt(HD)) + bias
            exponent = jnp.exp(scores - jnp.max(scores, axis=-1, keepdims=True))
            total = jnp.sum(exponent, axis=-1, keepdims=True)
            weights = (exponent / total).astype(jnp.bfloat16)
            att_all[q_rows, k_lanes] = jnp.dot(
                weights, values, preferred_element_type=jnp.float32
            ).astype(jnp.bfloat16)
        return carry

    lax.fori_loop(0, blocks, attend_block, 0)

    relay_step(1, half)
    for t in range(1, half + 1):
        finish_step(1, t)

    out_rows = wo_all.shape[0] * wo_all.shape[1]
    per_tile = 8
    out_tile = per_tile * wo_all.shape[1]

    for j in range(out_rows // out_tile):
        out_ref[:, pl.ds(j * out_tile, out_tile)] = lax.dot_general(
            att_all[...], wo_all[pl.ds(j * per_tile, per_tile)].reshape(out_tile, width),
            (((1,), (1,)), ((), ())), preferred_element_type=jnp.float32,
        ).astype(jnp.bfloat16)
    for copy in started:
        copy.wait_send()


def per_device_fused(tokens, w_qkv, w_out, key_blocks, key_levels):
    n = lax.axis_size("seq")
    own, model = tokens.shape
    blocks, list_len = key_blocks.shape
    width = HEADS * HD
    half = n // 2
    listed = blocks * list_len * QUART
    near = own + 2 * BLK
    w_rows = w_qkv.shape[0] // 4
    wo_rows = w_out.shape[1] // 4
    bf16 = jnp.bfloat16
    pair = lambda: pltpu.SemaphoreType.DMA((2, half, 2))
    vmem = pl.BlockSpec(memory_space=pltpu.VMEM)
    smem = pl.BlockSpec(memory_space=pltpu.SMEM)
    return pl.pallas_call(
        functools.partial(fused_kernel, n, blocks, list_len),
        out_shape=jax.ShapeDtypeStruct((own, model), bf16),
        in_specs=[smem, smem, vmem, vmem, vmem],
        out_specs=vmem,
        scratch_shapes=[
            pltpu.VMEM((n * 4, w_rows, 3 * width), bf16),
            pltpu.VMEM((n * 4, wo_rows, width), bf16),
            pltpu.VMEM((n * blocks, QUART, model), bf16),
            pltpu.VMEM((near + listed, model), bf16),
            pltpu.VMEM((own, width), bf16),
            pltpu.VMEM((near + listed, 2 * width), bf16),
            pltpu.VMEM((LANES, 2 * width), bf16),
            pltpu.VMEM((own, width), bf16),
            *[pair() for _ in range(8)],
            pltpu.SemaphoreType.DMA((half, 2)),
            pltpu.SemaphoreType.DMA((half, 2)),
            pltpu.SemaphoreType.DMA((2,)),
            pltpu.SemaphoreType.DMA((2,)),
        ],
        compiler_params=pltpu.CompilerParams(
            collective_id=0, has_side_effects=True, vmem_limit_bytes=56 * 1024 * 1024
        ),
    )(
        key_blocks, key_levels, tokens,
        w_qkv.reshape(4, w_rows, 3 * width), w_out.T.reshape(4, wo_rows, width),
    )


def per_device(tokens, w_qkv, w_out, key_blocks, key_levels):
    blocks, list_len = key_blocks.shape
    fits = (
        lax.axis_size("clip") == 4
        and lax.axis_size("seq") in (4, 6, 8)
        and w_qkv.shape[0] % 64 == 0
        and w_out.shape[1] % 64 == 0
        and blocks % 2 == 0
        and blocks * list_len <= LANES
        and (3 * BLK + list_len * QUART) % LANES == 0
    )
    form = per_device_fused if fits else per_device_general
    return form(tokens, w_qkv, w_out, key_blocks, key_levels)


def solution(mesh):
    placed = (
        P(("clip", "seq"), None),
        P("seq", None),
        P(None, "seq"),
        P(("clip", "seq"), None),
        P(("clip", "seq"), None),
    )
    return jax.shard_map(
        per_device, mesh=mesh, in_specs=placed, out_specs=P(("clip", "seq"), None), check_vma=False
    )
```

```python
import functools
import math

import jax
import jax.numpy as jnp
from jax import lax
from jax.experimental import pallas as pl
from jax.experimental.pallas import tpu as pltpu
from jax.sharding import PartitionSpec as P

HEADS = 6
HD = 128
BLK = 64
QUART = 16


masked_score = -1e30


def with_halo(block, sides, width):
    for axis, dim in sides:
        count = lax.axis_size(axis)
        forward = [(i, i + 1) for i in range(count - 1)]
        backward = [(target, source) for source, target in forward]
        low = lax.ppermute(
            lax.slice_in_dim(block, block.shape[dim] - width, None, axis=dim), axis, forward
        )
        high = lax.ppermute(lax.slice_in_dim(block, 0, width, axis=dim), axis, backward)
        block = jnp.concatenate([low, block, high], axis=dim)
    return block


def attend(queries, keys_all, score_bias, usable):
    block_count, key_count = (keys_all.shape[0], keys_all.shape[1])
    heads_view = keys_all.reshape(block_count, key_count, 2, HEADS, HD)
    scores = jnp.einsum(
        "bqhd,bkhd->bhqk", queries, heads_view[:, :, 0], preferred_element_type=jnp.float32
    )
    scores = scores * (1.0 / math.sqrt(HD)) + score_bias[:, None, None, :]
    scores = jnp.where(usable[:, None, None, :], scores, masked_score)
    row_top = jnp.max(scores, axis=-1, keepdims=True)
    exponent = jnp.exp(scores - row_top)
    total_mass = jnp.sum(exponent, axis=-1, keepdims=True)
    attn_weights = (exponent / total_mass).astype(jnp.bfloat16)
    attended = jnp.einsum(
        "bhqk,bkhd->bqhd", attn_weights, heads_view[:, :, 1], preferred_element_type=jnp.float32
    )
    return attended.astype(jnp.bfloat16)


def per_device_general(tokens, w_qkv, w_out, key_blocks, key_levels):
    peer_count = lax.axis_size("seq")
    own_index = lax.axis_index("seq")
    tok_rows = tokens.shape[0]
    local_blocks = tok_rows // BLK
    list_len = key_blocks.shape[1]
    slot_count = (local_blocks * list_len + peer_count - 1) // peer_count
    head_width = HEADS * HD
    projected = jnp.dot(
        tokens, lax.all_gather(w_qkv, "seq", axis=0, tiled=True), preferred_element_type=jnp.float32
    ).astype(jnp.bfloat16)
    queries = projected[:, :head_width]
    key_value = projected[:, head_width:]
    kv_blocks = key_value.reshape(local_blocks, BLK, 2 * head_width)
    widened = kv_blocks.astype(jnp.float32).reshape(
        local_blocks, QUART, BLK // QUART, 2 * head_width
    )
    coarse_own = jnp.mean(widened, axis=2).astype(jnp.bfloat16)
    flat_ids = key_blocks.reshape(-1)
    owner_ids = flat_ids // local_blocks
    local_ids = flat_ids % local_blocks
    peer_ids = jnp.arange(peer_count, dtype=jnp.int32)
    slot_ids = jnp.arange(slot_count, dtype=jnp.int32)
    owner_hot = (owner_ids[:, None] == peer_ids[None, :]).astype(jnp.int32)
    slot_rank = jnp.sum((jnp.cumsum(owner_hot, axis=0) - owner_hot) * owner_hot, axis=1)
    slot_hot = (slot_rank[:, None] == slot_ids[None, :]).astype(jnp.int32)
    wanted = jnp.sum(
        owner_hot[:, :, None] * slot_hot[:, None, :] * local_ids[:, None, None], axis=0
    )
    received = lax.all_to_all(
        coarse_own[lax.all_to_all(wanted, "seq", split_axis=0, concat_axis=0, tiled=True)],
        "seq",
        split_axis=0,
        concat_axis=0,
        tiled=True,
    )
    coarse_rows = received[owner_ids, slot_rank]
    single_rows = jnp.mean(coarse_rows.astype(jnp.float32), axis=1).astype(jnp.bfloat16)
    padded = with_halo(kv_blocks, (("seq", 0),), 1)
    near_rows = jnp.concatenate([padded[:-2], padded[1:-1], padded[2:]], axis=1)
    near_ids = (
        own_index * local_blocks
        + jnp.arange(local_blocks, dtype=jnp.int32)[:, None]
        + jnp.arange(3, dtype=jnp.int32)[None, :]
        - 1
    )
    near_ok = (near_ids >= 0) & (near_ids < local_blocks * peer_count)
    keys_all = jnp.concatenate(
        [
            near_rows,
            coarse_rows.reshape(local_blocks, list_len * QUART, 2 * head_width),
            single_rows.reshape(local_blocks, list_len, 2 * head_width),
        ],
        axis=1,
    )
    usable = jnp.concatenate(
        [
            jnp.repeat(near_ok, BLK, axis=1),
            jnp.repeat(key_levels == 1, QUART, axis=1),
            key_levels == 2,
        ],
        axis=1,
    )
    score_bias = jnp.concatenate(
        [
            jnp.zeros((local_blocks, 3 * BLK), jnp.float32),
            jnp.full((local_blocks, list_len * QUART), math.log(BLK / QUART), jnp.float32),
            jnp.full((local_blocks, list_len), math.log(BLK), jnp.float32),
        ],
        axis=1,
    )
    attended = attend(queries.reshape(local_blocks, BLK, HEADS, HD), keys_all, score_bias, usable)
    attended = attended.reshape(tok_rows, head_width)
    return jnp.dot(
        attended,
        lax.all_gather(w_out, "seq", axis=1, tiled=True),
        preferred_element_type=jnp.float32,
    ).astype(jnp.bfloat16)


MESH = pl.DeviceIdType.MESH
LANES = 128


def fused_kernel(
    n, blocks, list_len,
    blocks_ref, levels_ref, tok_ref, w_ref, wo_ref, out_ref,
    w_all, wo_all, c_all, rows_all, q_all, kv_all, pick_all, far_all, att_all,
    ring_send, ring_recv, core_send, core_recv, x_send, x_recv, relay_send, relay_recv,
    c_send, c_recv, halo_send, halo_recv,
):
    me = lax.axis_index("seq")
    clip = lax.axis_index("clip")
    half = n // 2
    own = blocks * BLK
    listed = blocks * list_len * QUART
    near = own + 2 * BLK
    width = HEADS * HD

    def owner_at(pos):
        pos = lax.rem(pos + 2 * n, n)
        return jnp.where(pos < half, 2 * pos, 2 * (n - 1 - pos) + 1)

    pos = jnp.where(lax.rem(me, 2) == 0, me // 2, n - 1 - me // 2)
    ring = ((owner_at(pos + 1), clip), (owner_at(pos - 1), clip))
    core_q = clip + 1 - 2 * lax.rem(clip, 2)
    x_q = lax.rem(clip + 2, 4)
    core_peer, x_peer = (me, core_q), (me, x_q)
    after, before = (lax.rem(me + 1, n), clip), (lax.rem(me + n - 1, n), clip)

    barrier = pltpu.get_barrier_semaphore()
    for peer in (*ring, core_peer, x_peer, after, before):
        pl.semaphore_signal(barrier, inc=1, device_id=peer, device_id_type=MESH)
    pl.semaphore_wait(barrier, 6)

    def remote(src, dst, send, recv, peer):
        return pltpu.make_async_remote_copy(
            src_ref=src, dst_ref=dst, send_sem=send, recv_sem=recv,
            device_id=peer, device_id_type=MESH,
        )

    started = []

    def start(copy):
        copy.start()
        started.append(copy)

    shards = ((w_ref, w_all), (wo_ref, wo_all))

    def part(ref, slot, t, way):
        lanes = ref.shape[-1]
        if t < half:
            return ref.at[slot]
        return ref.at[slot, :, pl.ds(way * (lanes // 2), lanes // 2)]

    def owner_from(t, way):
        return owner_at(pos - t) if way == 0 else owner_at(pos + t)

    def ring_send_step(kind, t):
        for way in range(2):
            source, full = shards[kind]
            owner = owner_from(t - 1, way)
            slot = owner * 4 + clip
            src = part(source, clip, t, way) if t == 1 else part(full, slot, t, way)
            start(remote(
                src, part(full, slot, t, way),
                ring_send.at[kind, t - 1, way], ring_recv.at[kind, t - 1, way], ring[way],
            ))

    def arrive(kind, t, way):
        full = shards[kind][1]
        mine = part(full, owner_from(t, way) * 4 + clip, t, way)
        remote(
            mine, mine, ring_send.at[kind, t - 1, way], ring_recv.at[kind, t - 1, way], ring[way]
        ).wait_recv()

    def share(kind, t):
        full = shards[kind][1]
        for way in range(2):
            mine = part(full, owner_from(t, way) * 4 + clip, t, way)
            at = (kind, t - 1, way)
            start(remote(mine, mine, x_send.at[at], x_recv.at[at], x_peer))
            start(remote(mine, mine, core_send.at[at], core_recv.at[at], core_peer))

    def ring_step(kind, t):
        for way in range(2):
            arrive(kind, t, way)
        if t < half:
            ring_send_step(kind, t + 1)
        share(kind, t)

    def relay_step(kind, t):
        full = shards[kind][1]
        for way in range(2):
            at = (kind, t - 1, way)
            theirs = part(full, owner_from(t, way) * 4 + x_q, t, way)
            remote(theirs, theirs, x_send.at[at], x_recv.at[at], x_peer).wait_recv()
            start(remote(theirs, theirs, relay_send.at[at], relay_recv.at[at], core_peer))

    def finish_step(kind, t):
        full = shards[kind][1]
        for way in range(2):
            at = (kind, t - 1, way)
            owner = owner_from(t, way)
            one = part(full, owner * 4 + core_q, t, way)
            remote(one, one, core_send.at[at], core_recv.at[at], core_peer).wait_recv()
            two = part(full, owner * 4 + lax.rem(core_q + 2, 4), t, way)
            remote(two, two, relay_send.at[at], relay_recv.at[at], core_peer).wait_recv()

    def c_part(owner, t, way):
        if t < half:
            return c_all.at[pl.ds(owner * blocks, blocks)]
        return c_all.at[pl.ds(owner * blocks + way * (blocks // 2), blocks // 2)]

    def c_send_step(t):
        for way in range(2):
            piece = c_part(owner_from(t - 1, way), t, way)
            start(remote(
                piece, piece, c_send.at[t - 1, way], c_recv.at[t - 1, way], ring[way]
            ))

    def c_step(t):
        for way in range(2):
            piece = c_part(owner_from(t, way), t, way)
            remote(
                piece, piece, c_send.at[t - 1, way], c_recv.at[t - 1, way], ring[way]
            ).wait_recv()
        if t < half:
            c_send_step(t + 1)

    ring_send_step(0, 1)
    coarse_count = blocks * QUART
    fold = BLK // QUART
    to_row = lax.broadcasted_iota(jnp.int32, (coarse_count, own), 0)
    from_row = lax.broadcasted_iota(jnp.int32, (coarse_count, own), 1)
    mean_of = jnp.where(
        (from_row >= to_row * fold) & (from_row < (to_row + 1) * fold), 1.0 / fold, 0.0
    ).astype(jnp.bfloat16)
    means = jnp.dot(mean_of, tok_ref[...], preferred_element_type=jnp.float32)
    c_all[pl.ds(me * blocks, blocks)] = means.astype(jnp.bfloat16).reshape(
        blocks, QUART, tok_ref.shape[1]
    )
    ring_step(0, 1)
    c_send_step(1)
    start(remote(
        tok_ref.at[pl.ds(own - BLK, BLK)], rows_all.at[pl.ds(0, BLK)],
        halo_send.at[0], halo_recv.at[0], after,
    ))
    start(remote(
        tok_ref.at[pl.ds(0, BLK)], rows_all.at[pl.ds(BLK + own, BLK)],
        halo_send.at[1], halo_recv.at[1], before,
    ))
    w_all[pl.ds(me * 4, 4)] = w_ref[...]
    wo_all[pl.ds(me * 4, 4)] = wo_ref[...]
    rows_all[pl.ds(BLK, own), :] = tok_ref[...]

    slab_row = lax.broadcasted_iota(jnp.int32, (QUART, listed), 0)
    slab_from = lax.broadcasted_iota(jnp.int32, (QUART, listed), 1)
    for b in range(blocks):
        for i in range(list_len):
            at = (b * list_len + i) * QUART
            level = levels_ref[i, b]
            inside = (slab_from >= at) & (slab_from < at + QUART)
            same = jnp.where(slab_from == slab_row + at, 1.0, 0.0)
            mean = jnp.where(inside, 1.0 / QUART, 0.0)
            pick_all[pl.ds(at, QUART), :] = jnp.where(
                (slab_row == 0) & (level == 2), mean, same
            ).astype(jnp.bfloat16)

    for t in range(2, half + 1):
        ring_step(0, t)
        relay_step(0, t - 1)
        if t < half:
            c_step(t - 1)
    for t in range(1, half):
        finish_step(0, t)
    relay_step(0, half)
    c_step(half - 1)
    ring_send_step(1, 1)
    finish_step(0, half)
    for low, high, side, peer in ((0, BLK, 0, after), (BLK + own, near, 1, before)):
        piece = rows_all.at[pl.ds(low, BLK)]
        remote(piece, piece, halo_send.at[side], halo_recv.at[side], peer).wait_recv()

    depth = w_all.shape[0] * w_all.shape[1]
    tile = 256

    def q_tile(j, carry):
        columns = pl.ds(pl.multiple_of(j * tile, tile), tile)
        q_all[:, columns] = jnp.dot(
            rows_all[pl.ds(BLK, own), :], w_all[:, :, columns].reshape(depth, tile),
            preferred_element_type=jnp.float32,
        ).astype(jnp.bfloat16)
        return carry

    def kv_tile(low, count, j, carry):
        columns = pl.ds(pl.multiple_of(j * tile, tile), tile)
        there = pl.ds(pl.multiple_of(width + j * tile, tile), tile)
        kv_all[pl.ds(low, count), columns] = jnp.dot(
            rows_all[pl.ds(low, count), :], w_all[:, :, there].reshape(depth, tile),
            preferred_element_type=jnp.float32,
        ).astype(jnp.bfloat16)
        return carry

    tiles = width // tile
    lax.fori_loop(0, tiles, q_tile, 0)
    lax.fori_loop(0, 2 * tiles, functools.partial(kv_tile, 0, near), 0)
    ring_step(1, 1)
    c_step(half)

    for b in range(blocks):
        for i in range(list_len):
            at = near + (b * list_len + i) * QUART
            rows_all[pl.ds(at, QUART), :] = c_all[blocks_ref[i, b]]
    lax.fori_loop(0, 2 * tiles, functools.partial(kv_tile, near, listed), 0)
    far_all[...] = jnp.dot(
        pick_all[...], kv_all[pl.ds(near, listed), :], preferred_element_type=jnp.float32
    ).astype(jnp.bfloat16)
    ring_step(1, 2)
    relay_step(1, 1)

    per = list_len * QUART
    key_count = 3 * BLK + per
    lane = lax.broadcasted_iota(jnp.int32, (1, key_count), 1)
    log2e = math.log2(math.e)

    def attend_block(b):
        bias = jnp.where(lane < 3 * BLK, 0.0, masked_score)
        bias = jnp.where((lane < BLK) & (me * blocks + b == 0), masked_score, bias)
        bias = jnp.where(
            (lane >= 2 * BLK) & (lane < 3 * BLK) & (me * blocks + b == n * blocks - 1),
            masked_score, bias,
        )
        for i in range(list_len):
            level = levels_ref[i, b]
            low = 3 * BLK + i * QUART
            bias = jnp.where(
                (lane >= low) & (lane < low + QUART) & (level == 1),
                math.log2(BLK / QUART), bias,
            )
            bias = jnp.where((lane == low) & (level == 2), math.log2(BLK), bias)
        q_rows = pl.ds(b * BLK, BLK)
        near_rows = pl.ds(b * BLK, 3 * BLK)
        far_rows = pl.ds(b * per, per)
        for h in range(HEADS):
            k_lanes = pl.ds(h * HD, HD)
            v_lanes = pl.ds(width + h * HD, HD)
            keys = jnp.concatenate([kv_all[near_rows, k_lanes], far_all[far_rows, k_lanes]], 0)
            values = jnp.concatenate([kv_all[near_rows, v_lanes], far_all[far_rows, v_lanes]], 0)
            scores = lax.dot_general(
                q_all[q_rows, k_lanes], keys, (((1,), (1,)), ((), ())),
                preferred_element_type=jnp.float32,
            )
            scores = scores * (log2e / math.sqrt(HD)) + bias
            exponent = jnp.exp2(scores - jnp.max(scores, axis=-1, keepdims=True))
            total = jnp.sum(exponent, axis=-1, keepdims=True)
            weights = (exponent * (1.0 / total)).astype(jnp.bfloat16)
            att_all[q_rows, k_lanes] = jnp.dot(
                weights, values, preferred_element_type=jnp.float32
            ).astype(jnp.bfloat16)

    for b in range(blocks):
        attend_block(b)
        t = 3 + b
        if t <= half:
            ring_step(1, t)
            relay_step(1, t - 1)
        elif t == half + 1:
            relay_step(1, half)
    for t in range(1, half + 1):
        finish_step(1, t)

    per_tile = 8
    out_tile = per_tile * wo_all.shape[1]
    for j in range(wo_all.shape[0] // per_tile):
        out_ref[:, pl.ds(j * out_tile, out_tile)] = lax.dot_general(
            att_all[...], wo_all[pl.ds(j * per_tile, per_tile)].reshape(out_tile, width),
            (((1,), (1,)), ((), ())), preferred_element_type=jnp.float32,
        ).astype(jnp.bfloat16)
    for copy in started:
        copy.wait_send()


def per_device_fused(tokens, w_qkv, w_out, key_blocks, key_levels):
    n = lax.axis_size("seq")
    own, model = tokens.shape
    blocks, list_len = key_blocks.shape
    width = HEADS * HD
    half = n // 2
    listed = blocks * list_len * QUART
    near = own + 2 * BLK
    w_rows = w_qkv.shape[0] // 4
    wo_rows = w_out.shape[1] // 4
    bf16 = jnp.bfloat16
    pair = lambda: pltpu.SemaphoreType.DMA((2, half, 2))
    vmem = pl.BlockSpec(memory_space=pltpu.VMEM)
    smem = pl.BlockSpec(memory_space=pltpu.SMEM)
    return pl.pallas_call(
        functools.partial(fused_kernel, n, blocks, list_len),
        out_shape=jax.ShapeDtypeStruct((own, model), bf16),
        in_specs=[smem, smem, vmem, vmem, vmem],
        out_specs=vmem,
        scratch_shapes=[
            pltpu.VMEM((n * 4, w_rows, 3 * width), bf16),
            pltpu.VMEM((n * 4, wo_rows, width), bf16),
            pltpu.VMEM((n * blocks, QUART, model), bf16),
            pltpu.VMEM((near + listed, model), bf16),
            pltpu.VMEM((own, width), bf16),
            pltpu.VMEM((near + listed, 2 * width), bf16),
            pltpu.VMEM((listed, listed), bf16),
            pltpu.VMEM((listed, 2 * width), bf16),
            pltpu.VMEM((own, width), bf16),
            *[pair() for _ in range(8)],
            pltpu.SemaphoreType.DMA((half, 2)),
            pltpu.SemaphoreType.DMA((half, 2)),
            pltpu.SemaphoreType.DMA((2,)),
            pltpu.SemaphoreType.DMA((2,)),
        ],
        compiler_params=pltpu.CompilerParams(
            collective_id=0, has_side_effects=True, vmem_limit_bytes=56 * 1024 * 1024
        ),
    )(
        key_blocks.T, key_levels.T, tokens,
        w_qkv.reshape(4, w_rows, 3 * width), w_out.T.reshape(4, wo_rows, width),
    )


def per_device(tokens, w_qkv, w_out, key_blocks, key_levels):
    blocks, list_len = key_blocks.shape
    fits = (
        lax.axis_size("clip") == 4
        and lax.axis_size("seq") in (4, 6, 8)
        and w_qkv.shape[0] % 64 == 0
        and w_out.shape[1] % 64 == 0
        and blocks % 2 == 0
        and blocks >= 4
        and (3 * BLK + list_len * QUART) % LANES == 0
    )
    form = per_device_fused if fits else per_device_general
    return form(tokens, w_qkv, w_out, key_blocks, key_levels)


def solution(mesh):
    placed = (
        P(("clip", "seq"), None),
        P("seq", None),
        P(None, "seq"),
        P(("clip", "seq"), None),
        P(("clip", "seq"), None),
    )
    return jax.shard_map(
        per_device, mesh=mesh, in_specs=placed, out_specs=P(("clip", "seq"), None), check_vma=False
    )
```

```python
import functools
import math

import jax
import jax.numpy as jnp
from jax import lax
from jax.experimental import pallas as pl
from jax.experimental.pallas import tpu as pltpu
from jax.sharding import PartitionSpec as P

HEADS = 6
HD = 128
BLK = 64
QUART = 16


masked_score = -1e30


def with_halo(block, sides, width):
    for axis, dim in sides:
        count = lax.axis_size(axis)
        forward = [(i, i + 1) for i in range(count - 1)]
        backward = [(target, source) for source, target in forward]
        low = lax.ppermute(
            lax.slice_in_dim(block, block.shape[dim] - width, None, axis=dim), axis, forward
        )
        high = lax.ppermute(lax.slice_in_dim(block, 0, width, axis=dim), axis, backward)
        block = jnp.concatenate([low, block, high], axis=dim)
    return block


def attend(queries, keys_all, score_bias, usable):
    block_count, key_count = (keys_all.shape[0], keys_all.shape[1])
    heads_view = keys_all.reshape(block_count, key_count, 2, HEADS, HD)
    scores = jnp.einsum(
        "bqhd,bkhd->bhqk", queries, heads_view[:, :, 0], preferred_element_type=jnp.float32
    )
    scores = scores * (1.0 / math.sqrt(HD)) + score_bias[:, None, None, :]
    scores = jnp.where(usable[:, None, None, :], scores, masked_score)
    row_top = jnp.max(scores, axis=-1, keepdims=True)
    exponent = jnp.exp(scores - row_top)
    total_mass = jnp.sum(exponent, axis=-1, keepdims=True)
    attn_weights = (exponent / total_mass).astype(jnp.bfloat16)
    attended = jnp.einsum(
        "bhqk,bkhd->bqhd", attn_weights, heads_view[:, :, 1], preferred_element_type=jnp.float32
    )
    return attended.astype(jnp.bfloat16)


def per_device_general(tokens, w_qkv, w_out, key_blocks, key_levels):
    peer_count = lax.axis_size("seq")
    own_index = lax.axis_index("seq")
    tok_rows = tokens.shape[0]
    local_blocks = tok_rows // BLK
    list_len = key_blocks.shape[1]
    slot_count = (local_blocks * list_len + peer_count - 1) // peer_count
    head_width = HEADS * HD
    projected = jnp.dot(
        tokens, lax.all_gather(w_qkv, "seq", axis=0, tiled=True), preferred_element_type=jnp.float32
    ).astype(jnp.bfloat16)
    queries = projected[:, :head_width]
    key_value = projected[:, head_width:]
    kv_blocks = key_value.reshape(local_blocks, BLK, 2 * head_width)
    widened = kv_blocks.astype(jnp.float32).reshape(
        local_blocks, QUART, BLK // QUART, 2 * head_width
    )
    coarse_own = jnp.mean(widened, axis=2).astype(jnp.bfloat16)
    flat_ids = key_blocks.reshape(-1)
    owner_ids = flat_ids // local_blocks
    local_ids = flat_ids % local_blocks
    peer_ids = jnp.arange(peer_count, dtype=jnp.int32)
    slot_ids = jnp.arange(slot_count, dtype=jnp.int32)
    owner_hot = (owner_ids[:, None] == peer_ids[None, :]).astype(jnp.int32)
    slot_rank = jnp.sum((jnp.cumsum(owner_hot, axis=0) - owner_hot) * owner_hot, axis=1)
    slot_hot = (slot_rank[:, None] == slot_ids[None, :]).astype(jnp.int32)
    wanted = jnp.sum(
        owner_hot[:, :, None] * slot_hot[:, None, :] * local_ids[:, None, None], axis=0
    )
    received = lax.all_to_all(
        coarse_own[lax.all_to_all(wanted, "seq", split_axis=0, concat_axis=0, tiled=True)],
        "seq",
        split_axis=0,
        concat_axis=0,
        tiled=True,
    )
    coarse_rows = received[owner_ids, slot_rank]
    single_rows = jnp.mean(coarse_rows.astype(jnp.float32), axis=1).astype(jnp.bfloat16)
    padded = with_halo(kv_blocks, (("seq", 0),), 1)
    near_rows = jnp.concatenate([padded[:-2], padded[1:-1], padded[2:]], axis=1)
    near_ids = (
        own_index * local_blocks
        + jnp.arange(local_blocks, dtype=jnp.int32)[:, None]
        + jnp.arange(3, dtype=jnp.int32)[None, :]
        - 1
    )
    near_ok = (near_ids >= 0) & (near_ids < local_blocks * peer_count)
    keys_all = jnp.concatenate(
        [
            near_rows,
            coarse_rows.reshape(local_blocks, list_len * QUART, 2 * head_width),
            single_rows.reshape(local_blocks, list_len, 2 * head_width),
        ],
        axis=1,
    )
    usable = jnp.concatenate(
        [
            jnp.repeat(near_ok, BLK, axis=1),
            jnp.repeat(key_levels == 1, QUART, axis=1),
            key_levels == 2,
        ],
        axis=1,
    )
    score_bias = jnp.concatenate(
        [
            jnp.zeros((local_blocks, 3 * BLK), jnp.float32),
            jnp.full((local_blocks, list_len * QUART), math.log(BLK / QUART), jnp.float32),
            jnp.full((local_blocks, list_len), math.log(BLK), jnp.float32),
        ],
        axis=1,
    )
    attended = attend(queries.reshape(local_blocks, BLK, HEADS, HD), keys_all, score_bias, usable)
    attended = attended.reshape(tok_rows, head_width)
    return jnp.dot(
        attended,
        lax.all_gather(w_out, "seq", axis=1, tiled=True),
        preferred_element_type=jnp.float32,
    ).astype(jnp.bfloat16)


MESH = pl.DeviceIdType.MESH
LANES = 128


def fused_kernel(
    n, blocks, list_len,
    blocks_ref, levels_ref, tok_ref, w_ref, wo_ref, out_ref,
    w_all, wo_all, c_all, rows_all, q_all, kv_all, pick_all, far_all, att_all,
    ring_send, ring_recv, core_send, core_recv, x_send, x_recv, relay_send, relay_recv,
    c_send, c_recv, halo_send, halo_recv,
):
    me = lax.axis_index("seq")
    clip = lax.axis_index("clip")
    half = n // 2
    own = blocks * BLK
    listed = blocks * list_len * QUART
    near = own + 2 * BLK
    width = HEADS * HD

    def owner_at(pos):
        pos = lax.rem(pos + 2 * n, n)
        return jnp.where(pos < half, 2 * pos, 2 * (n - 1 - pos) + 1)

    pos = jnp.where(lax.rem(me, 2) == 0, me // 2, n - 1 - me // 2)
    ring = ((owner_at(pos + 1), clip), (owner_at(pos - 1), clip))
    core_q = clip + 1 - 2 * lax.rem(clip, 2)
    x_q = lax.rem(clip + 2, 4)
    core_peer, x_peer = (me, core_q), (me, x_q)
    after, before = (lax.rem(me + 1, n), clip), (lax.rem(me + n - 1, n), clip)

    barrier = pltpu.get_barrier_semaphore()
    for peer in (*ring, core_peer, x_peer, after, before):
        pl.semaphore_signal(barrier, inc=1, device_id=peer, device_id_type=MESH)

    def remote(src, dst, send, recv, peer):
        return pltpu.make_async_remote_copy(
            src_ref=src, dst_ref=dst, send_sem=send, recv_sem=recv,
            device_id=peer, device_id_type=MESH,
        )

    started = []

    def start(copy):
        copy.start()
        started.append(copy)

    shards = ((w_ref, w_all), (wo_ref, wo_all))

    def part(ref, slot, t, way):
        lanes = ref.shape[-1]
        if t < half:
            return ref.at[slot]
        return ref.at[slot, :, pl.ds(way * (lanes // 2), lanes // 2)]

    def owner_from(t, way):
        return owner_at(pos - t) if way == 0 else owner_at(pos + t)

    def ring_send_step(kind, t):
        for way in range(2):
            source, full = shards[kind]
            owner = owner_from(t - 1, way)
            slot = owner * 4 + clip
            src = part(source, clip, t, way) if t == 1 else part(full, slot, t, way)
            start(remote(
                src, part(full, slot, t, way),
                ring_send.at[kind, t - 1, way], ring_recv.at[kind, t - 1, way], ring[way],
            ))

    def arrive(kind, t, way):
        full = shards[kind][1]
        mine = part(full, owner_from(t, way) * 4 + clip, t, way)
        remote(
            mine, mine, ring_send.at[kind, t - 1, way], ring_recv.at[kind, t - 1, way], ring[way]
        ).wait_recv()

    def share(kind, t):
        full = shards[kind][1]
        for way in range(2):
            mine = part(full, owner_from(t, way) * 4 + clip, t, way)
            at = (kind, t - 1, way)
            start(remote(mine, mine, x_send.at[at], x_recv.at[at], x_peer))
            start(remote(mine, mine, core_send.at[at], core_recv.at[at], core_peer))

    def ring_step(kind, t):
        for way in range(2):
            arrive(kind, t, way)
        if t < half:
            ring_send_step(kind, t + 1)
        share(kind, t)

    def relay_step(kind, t):
        full = shards[kind][1]
        for way in range(2):
            at = (kind, t - 1, way)
            theirs = part(full, owner_from(t, way) * 4 + x_q, t, way)
            remote(theirs, theirs, x_send.at[at], x_recv.at[at], x_peer).wait_recv()
            start(remote(theirs, theirs, relay_send.at[at], relay_recv.at[at], core_peer))

    def finish_step(kind, t):
        full = shards[kind][1]
        for way in range(2):
            at = (kind, t - 1, way)
            owner = owner_from(t, way)
            one = part(full, owner * 4 + core_q, t, way)
            remote(one, one, core_send.at[at], core_recv.at[at], core_peer).wait_recv()
            two = part(full, owner * 4 + lax.rem(core_q + 2, 4), t, way)
            remote(two, two, relay_send.at[at], relay_recv.at[at], core_peer).wait_recv()

    def c_part(owner, t, way):
        if t < half:
            return c_all.at[pl.ds(owner * blocks, blocks)]
        return c_all.at[pl.ds(owner * blocks + way * (blocks // 2), blocks // 2)]

    def c_send_step(t):
        for way in range(2):
            piece = c_part(owner_from(t - 1, way), t, way)
            start(remote(
                piece, piece, c_send.at[t - 1, way], c_recv.at[t - 1, way], ring[way]
            ))

    def c_step(t):
        for way in range(2):
            piece = c_part(owner_from(t, way), t, way)
            remote(
                piece, piece, c_send.at[t - 1, way], c_recv.at[t - 1, way], ring[way]
            ).wait_recv()
        if t < half:
            c_send_step(t + 1)

    coarse_count = blocks * QUART
    fold = BLK // QUART
    to_row = lax.broadcasted_iota(jnp.int32, (coarse_count, own), 0)
    from_row = lax.broadcasted_iota(jnp.int32, (coarse_count, own), 1)
    mean_of = jnp.where(
        (from_row >= to_row * fold) & (from_row < (to_row + 1) * fold), 1.0 / fold, 0.0
    ).astype(jnp.bfloat16)
    means = jnp.dot(mean_of, tok_ref[...], preferred_element_type=jnp.float32)
    c_all[pl.ds(me * blocks, blocks)] = means.astype(jnp.bfloat16).reshape(
        blocks, QUART, tok_ref.shape[1]
    )
    w_all[pl.ds(me * 4, 4)] = w_ref[...]
    wo_all[pl.ds(me * 4, 4)] = wo_ref[...]
    rows_all[pl.ds(BLK, own), :] = tok_ref[...]

    slab_row = lax.broadcasted_iota(jnp.int32, (QUART, listed), 0)
    slab_from = lax.broadcasted_iota(jnp.int32, (QUART, listed), 1)
    for b in range(blocks):
        for i in range(list_len):
            at = (b * list_len + i) * QUART
            level = levels_ref[i, b]
            inside = (slab_from >= at) & (slab_from < at + QUART)
            same = jnp.where(slab_from == slab_row + at, 1.0, 0.0)
            mean = jnp.where(inside, 1.0 / QUART, 0.0)
            pick_all[pl.ds(at, QUART), :] = jnp.where(
                (slab_row == 0) & (level == 2), mean, same
            ).astype(jnp.bfloat16)

    first, last = me == 0, me == n - 1

    @pl.when(first)
    def _():
        rows_all[pl.ds(0, BLK), :] = jnp.zeros((BLK, rows_all.shape[1]), jnp.bfloat16)

    @pl.when(last)
    def _():
        rows_all[pl.ds(BLK + own, BLK), :] = jnp.zeros((BLK, rows_all.shape[1]), jnp.bfloat16)

    pl.semaphore_wait(barrier, 6)

    ring_send_step(0, 1)
    ring_step(0, 1)
    c_send_step(1)
    up = remote(
        tok_ref.at[pl.ds(own - BLK, BLK)], rows_all.at[pl.ds(0, BLK)],
        halo_send.at[0], halo_recv.at[0], after,
    )
    down = remote(
        tok_ref.at[pl.ds(0, BLK)], rows_all.at[pl.ds(BLK + own, BLK)],
        halo_send.at[1], halo_recv.at[1], before,
    )
    pl.when(me < n - 1)(up.start)
    pl.when(me > 0)(down.start)
    for t in range(2, half + 1):
        ring_step(0, t)
        relay_step(0, t - 1)
        if t == 2:
            ring_send_step(1, 1)
        else:
            ring_step(1, t - 2)
            if t > 3:
                relay_step(1, t - 3)
        if t < half:
            c_step(t - 1)
    for t in range(1, half):
        finish_step(0, t)
    relay_step(0, half)
    c_step(half - 1)
    finish_step(0, half)
    pl.when(me > 0)(up.wait_recv)
    pl.when(me < n - 1)(down.wait_recv)

    depth = w_all.shape[0] * w_all.shape[1]
    tile = 256

    def q_tile(j, carry):
        columns = pl.ds(pl.multiple_of(j * tile, tile), tile)
        q_all[:, columns] = jnp.dot(
            rows_all[pl.ds(BLK, own), :], w_all[:, :, columns].reshape(depth, tile),
            preferred_element_type=jnp.float32,
        ).astype(jnp.bfloat16)
        return carry

    def kv_tile(low, count, j, carry):
        columns = pl.ds(pl.multiple_of(j * tile, tile), tile)
        there = pl.ds(pl.multiple_of(width + j * tile, tile), tile)
        kv_all[pl.ds(low, count), columns] = jnp.dot(
            rows_all[pl.ds(low, count), :], w_all[:, :, there].reshape(depth, tile),
            preferred_element_type=jnp.float32,
        ).astype(jnp.bfloat16)
        return carry

    tiles = width // tile
    lax.fori_loop(0, tiles, q_tile, 0)
    lax.fori_loop(0, 2 * tiles, functools.partial(kv_tile, 0, near), 0)
    ring_step(1, half - 1)
    relay_step(1, half - 2)
    c_step(half)

    for b in range(blocks):
        for i in range(list_len):
            at = near + (b * list_len + i) * QUART
            rows_all[pl.ds(at, QUART), :] = c_all[blocks_ref[i, b]]
    lax.fori_loop(0, 2 * tiles, functools.partial(kv_tile, near, listed), 0)
    far_all[...] = jnp.dot(
        pick_all[...], kv_all[pl.ds(near, listed), :], preferred_element_type=jnp.float32
    ).astype(jnp.bfloat16)
    ring_step(1, half)
    relay_step(1, half - 1)

    per = list_len * QUART
    key_count = 3 * BLK + per
    lane = lax.broadcasted_iota(jnp.int32, (1, key_count), 1)
    log2e = math.log2(math.e)

    def attend_block(b):
        bias = jnp.where(lane < 3 * BLK, 0.0, masked_score)
        bias = jnp.where((lane < BLK) & (me * blocks + b == 0), masked_score, bias)
        bias = jnp.where(
            (lane >= 2 * BLK) & (lane < 3 * BLK) & (me * blocks + b == n * blocks - 1),
            masked_score, bias,
        )
        for i in range(list_len):
            level = levels_ref[i, b]
            low = 3 * BLK + i * QUART
            bias = jnp.where(
                (lane >= low) & (lane < low + QUART) & (level == 1),
                math.log2(BLK / QUART), bias,
            )
            bias = jnp.where((lane == low) & (level == 2), math.log2(BLK), bias)
        q_rows = pl.ds(b * BLK, BLK)
        near_rows = pl.ds(b * BLK, 3 * BLK)
        far_rows = pl.ds(b * per, per)
        for h in range(HEADS):
            k_lanes = pl.ds(h * HD, HD)
            v_lanes = pl.ds(width + h * HD, HD)
            keys = jnp.concatenate([kv_all[near_rows, k_lanes], far_all[far_rows, k_lanes]], 0)
            values = jnp.concatenate([kv_all[near_rows, v_lanes], far_all[far_rows, v_lanes]], 0)
            scores = lax.dot_general(
                q_all[q_rows, k_lanes], keys, (((1,), (1,)), ((), ())),
                preferred_element_type=jnp.float32,
            )
            scores = scores * (log2e / math.sqrt(HD)) + bias
            exponent = jnp.exp2(scores - jnp.max(scores, axis=-1, keepdims=True))
            total = jnp.sum(exponent, axis=-1, keepdims=True)
            weights = (exponent * (1.0 / total)).astype(jnp.bfloat16)
            att_all[q_rows, k_lanes] = jnp.dot(
                weights, values, preferred_element_type=jnp.float32
            ).astype(jnp.bfloat16)

    for b in range(blocks):
        attend_block(b)
        if b == 2:
            relay_step(1, half)
    for t in range(1, half + 1):
        finish_step(1, t)

    per_tile = 8
    out_tile = per_tile * wo_all.shape[1]
    for j in range(wo_all.shape[0] // per_tile):
        out_ref[:, pl.ds(j * out_tile, out_tile)] = lax.dot_general(
            att_all[...], wo_all[pl.ds(j * per_tile, per_tile)].reshape(out_tile, width),
            (((1,), (1,)), ((), ())), preferred_element_type=jnp.float32,
        ).astype(jnp.bfloat16)
    pl.when(me < n - 1)(up.wait_send)
    pl.when(me > 0)(down.wait_send)
    for copy in started:
        copy.wait_send()


def per_device_fused(tokens, w_qkv, w_out, key_blocks, key_levels):
    n = lax.axis_size("seq")
    own, model = tokens.shape
    blocks, list_len = key_blocks.shape
    width = HEADS * HD
    half = n // 2
    listed = blocks * list_len * QUART
    near = own + 2 * BLK
    w_rows = w_qkv.shape[0] // 4
    wo_rows = w_out.shape[1] // 4
    bf16 = jnp.bfloat16
    pair = lambda: pltpu.SemaphoreType.DMA((2, half, 2))
    vmem = pl.BlockSpec(memory_space=pltpu.VMEM)
    smem = pl.BlockSpec(memory_space=pltpu.SMEM)
    return pl.pallas_call(
        functools.partial(fused_kernel, n, blocks, list_len),
        out_shape=jax.ShapeDtypeStruct((own, model), bf16),
        in_specs=[smem, smem, vmem, vmem, vmem],
        out_specs=vmem,
        scratch_shapes=[
            pltpu.VMEM((n * 4, w_rows, 3 * width), bf16),
            pltpu.VMEM((n * 4, wo_rows, width), bf16),
            pltpu.VMEM((n * blocks, QUART, model), bf16),
            pltpu.VMEM((near + listed, model), bf16),
            pltpu.VMEM((own, width), bf16),
            pltpu.VMEM((near + listed, 2 * width), bf16),
            pltpu.VMEM((listed, listed), bf16),
            pltpu.VMEM((listed, 2 * width), bf16),
            pltpu.VMEM((own, width), bf16),
            *[pair() for _ in range(8)],
            pltpu.SemaphoreType.DMA((half, 2)),
            pltpu.SemaphoreType.DMA((half, 2)),
            pltpu.SemaphoreType.DMA((2,)),
            pltpu.SemaphoreType.DMA((2,)),
        ],
        compiler_params=pltpu.CompilerParams(
            collective_id=0, has_side_effects=True, vmem_limit_bytes=56 * 1024 * 1024
        ),
    )(
        key_blocks.T, key_levels.T, tokens,
        w_qkv.reshape(4, w_rows, 3 * width), w_out.T.reshape(4, wo_rows, width),
    )


def per_device(tokens, w_qkv, w_out, key_blocks, key_levels):
    blocks, list_len = key_blocks.shape
    fits = (
        lax.axis_size("clip") == 4
        and lax.axis_size("seq") in (4, 6, 8)
        and w_qkv.shape[0] % 64 == 0
        and w_out.shape[1] % 64 == 0
        and blocks % 2 == 0
        and blocks >= 4
        and (3 * BLK + list_len * QUART) % LANES == 0
    )
    form = per_device_fused if fits else per_device_general
    return form(tokens, w_qkv, w_out, key_blocks, key_levels)


def solution(mesh):
    placed = (
        P(("clip", "seq"), None),
        P("seq", None),
        P(None, "seq"),
        P(("clip", "seq"), None),
        P(("clip", "seq"), None),
    )
    return jax.shard_map(
        per_device, mesh=mesh, in_specs=placed, out_specs=P(("clip", "seq"), None), check_vma=False
    )
```

```python
import functools
import math

import jax
import jax.numpy as jnp
from jax import lax
from jax.experimental import pallas as pl
from jax.experimental.pallas import tpu as pltpu
from jax.sharding import PartitionSpec as P

HEADS = 6
HD = 128
BLK = 64
QUART = 16


masked_score = -1e30


def with_halo(block, sides, width):
    for axis, dim in sides:
        count = lax.axis_size(axis)
        forward = [(i, i + 1) for i in range(count - 1)]
        backward = [(target, source) for source, target in forward]
        low = lax.ppermute(
            lax.slice_in_dim(block, block.shape[dim] - width, None, axis=dim), axis, forward
        )
        high = lax.ppermute(lax.slice_in_dim(block, 0, width, axis=dim), axis, backward)
        block = jnp.concatenate([low, block, high], axis=dim)
    return block


def attend(queries, keys_all, score_bias, usable):
    block_count, key_count = (keys_all.shape[0], keys_all.shape[1])
    heads_view = keys_all.reshape(block_count, key_count, 2, HEADS, HD)
    scores = jnp.einsum(
        "bqhd,bkhd->bhqk", queries, heads_view[:, :, 0], preferred_element_type=jnp.float32
    )
    scores = scores * (1.0 / math.sqrt(HD)) + score_bias[:, None, None, :]
    scores = jnp.where(usable[:, None, None, :], scores, masked_score)
    row_top = jnp.max(scores, axis=-1, keepdims=True)
    exponent = jnp.exp(scores - row_top)
    total_mass = jnp.sum(exponent, axis=-1, keepdims=True)
    attn_weights = (exponent / total_mass).astype(jnp.bfloat16)
    attended = jnp.einsum(
        "bhqk,bkhd->bqhd", attn_weights, heads_view[:, :, 1], preferred_element_type=jnp.float32
    )
    return attended.astype(jnp.bfloat16)


def per_device_general(tokens, w_qkv, w_out, key_blocks, key_levels):
    peer_count = lax.axis_size("seq")
    own_index = lax.axis_index("seq")
    tok_rows = tokens.shape[0]
    local_blocks = tok_rows // BLK
    list_len = key_blocks.shape[1]
    slot_count = (local_blocks * list_len + peer_count - 1) // peer_count
    head_width = HEADS * HD
    projected = jnp.dot(
        tokens, lax.all_gather(w_qkv, "seq", axis=0, tiled=True), preferred_element_type=jnp.float32
    ).astype(jnp.bfloat16)
    queries = projected[:, :head_width]
    key_value = projected[:, head_width:]
    kv_blocks = key_value.reshape(local_blocks, BLK, 2 * head_width)
    widened = kv_blocks.astype(jnp.float32).reshape(
        local_blocks, QUART, BLK // QUART, 2 * head_width
    )
    coarse_own = jnp.mean(widened, axis=2).astype(jnp.bfloat16)
    flat_ids = key_blocks.reshape(-1)
    owner_ids = flat_ids // local_blocks
    local_ids = flat_ids % local_blocks
    peer_ids = jnp.arange(peer_count, dtype=jnp.int32)
    slot_ids = jnp.arange(slot_count, dtype=jnp.int32)
    owner_hot = (owner_ids[:, None] == peer_ids[None, :]).astype(jnp.int32)
    slot_rank = jnp.sum((jnp.cumsum(owner_hot, axis=0) - owner_hot) * owner_hot, axis=1)
    slot_hot = (slot_rank[:, None] == slot_ids[None, :]).astype(jnp.int32)
    wanted = jnp.sum(
        owner_hot[:, :, None] * slot_hot[:, None, :] * local_ids[:, None, None], axis=0
    )
    received = lax.all_to_all(
        coarse_own[lax.all_to_all(wanted, "seq", split_axis=0, concat_axis=0, tiled=True)],
        "seq",
        split_axis=0,
        concat_axis=0,
        tiled=True,
    )
    coarse_rows = received[owner_ids, slot_rank]
    single_rows = jnp.mean(coarse_rows.astype(jnp.float32), axis=1).astype(jnp.bfloat16)
    padded = with_halo(kv_blocks, (("seq", 0),), 1)
    near_rows = jnp.concatenate([padded[:-2], padded[1:-1], padded[2:]], axis=1)
    near_ids = (
        own_index * local_blocks
        + jnp.arange(local_blocks, dtype=jnp.int32)[:, None]
        + jnp.arange(3, dtype=jnp.int32)[None, :]
        - 1
    )
    near_ok = (near_ids >= 0) & (near_ids < local_blocks * peer_count)
    keys_all = jnp.concatenate(
        [
            near_rows,
            coarse_rows.reshape(local_blocks, list_len * QUART, 2 * head_width),
            single_rows.reshape(local_blocks, list_len, 2 * head_width),
        ],
        axis=1,
    )
    usable = jnp.concatenate(
        [
            jnp.repeat(near_ok, BLK, axis=1),
            jnp.repeat(key_levels == 1, QUART, axis=1),
            key_levels == 2,
        ],
        axis=1,
    )
    score_bias = jnp.concatenate(
        [
            jnp.zeros((local_blocks, 3 * BLK), jnp.float32),
            jnp.full((local_blocks, list_len * QUART), math.log(BLK / QUART), jnp.float32),
            jnp.full((local_blocks, list_len), math.log(BLK), jnp.float32),
        ],
        axis=1,
    )
    attended = attend(queries.reshape(local_blocks, BLK, HEADS, HD), keys_all, score_bias, usable)
    attended = attended.reshape(tok_rows, head_width)
    return jnp.dot(
        attended,
        lax.all_gather(w_out, "seq", axis=1, tiled=True),
        preferred_element_type=jnp.float32,
    ).astype(jnp.bfloat16)


MESH = pl.DeviceIdType.MESH
LANES = 128


def fused_kernel(
    n, blocks, list_len,
    blocks_ref, levels_ref, tok_ref, w_ref, wo_ref, out_ref,
    w_all, wo_all, c_all, rows_all, q_all, kv_all, pick_all, far_all, att_all,
    ring_send, ring_recv, core_send, core_recv, x_send, x_recv, relay_send, relay_recv,
    c_send, c_recv, halo_send, halo_recv,
):
    me = lax.axis_index("seq")
    clip = lax.axis_index("clip")
    half = n // 2
    own = blocks * BLK
    listed = blocks * list_len * QUART
    near = own + 2 * BLK
    width = HEADS * HD

    def owner_at(pos):
        pos = lax.rem(pos + 2 * n, n)
        return jnp.where(pos < half, 2 * pos, 2 * (n - 1 - pos) + 1)

    pos = jnp.where(lax.rem(me, 2) == 0, me // 2, n - 1 - me // 2)
    ring = ((owner_at(pos + 1), clip), (owner_at(pos - 1), clip))
    core_q = clip + 1 - 2 * lax.rem(clip, 2)
    x_q = lax.rem(clip + 2, 4)
    core_peer, x_peer = (me, core_q), (me, x_q)
    after, before = (lax.rem(me + 1, n), clip), (lax.rem(me + n - 1, n), clip)

    barrier = pltpu.get_barrier_semaphore()
    for peer in (*ring, core_peer, x_peer, after, before):
        pl.semaphore_signal(barrier, inc=1, device_id=peer, device_id_type=MESH)

    def remote(src, dst, send, recv, peer):
        return pltpu.make_async_remote_copy(
            src_ref=src, dst_ref=dst, send_sem=send, recv_sem=recv,
            device_id=peer, device_id_type=MESH,
        )

    started = []

    def start(copy):
        copy.start()
        started.append(copy)

    shards = ((w_ref, w_all), (wo_ref, wo_all))

    def part(ref, slot, t, way):
        lanes = ref.shape[-1]
        if t < half:
            return ref.at[slot]
        return ref.at[slot, :, pl.ds(way * (lanes // 2), lanes // 2)]

    def owner_from(t, way):
        return owner_at(pos - t) if way == 0 else owner_at(pos + t)

    def ring_send_step(kind, t, ways=(0, 1)):
        for way in ways:
            source, full = shards[kind]
            owner = owner_from(t - 1, way)
            slot = owner * 4 + clip
            src = part(source, clip, t, way) if t == 1 else part(full, slot, t, way)
            start(remote(
                src, part(full, slot, t, way),
                ring_send.at[kind, t - 1, way], ring_recv.at[kind, t - 1, way], ring[way],
            ))

    def arrive(kind, t, way):
        full = shards[kind][1]
        mine = part(full, owner_from(t, way) * 4 + clip, t, way)
        remote(
            mine, mine, ring_send.at[kind, t - 1, way], ring_recv.at[kind, t - 1, way], ring[way]
        ).wait_recv()

    def share(kind, t, ways=(0, 1)):
        full = shards[kind][1]
        for way in ways:
            mine = part(full, owner_from(t, way) * 4 + clip, t, way)
            at = (kind, t - 1, way)
            start(remote(mine, mine, x_send.at[at], x_recv.at[at], x_peer))
            start(remote(mine, mine, core_send.at[at], core_recv.at[at], core_peer))

    def ring_step(kind, t):
        for way in range(2):
            arrive(kind, t, way)
            if t < half:
                ring_send_step(kind, t + 1, (way,))
            share(kind, t, (way,))

    def relay_step(kind, t):
        full = shards[kind][1]
        for way in range(2):
            at = (kind, t - 1, way)
            theirs = part(full, owner_from(t, way) * 4 + x_q, t, way)
            remote(theirs, theirs, x_send.at[at], x_recv.at[at], x_peer).wait_recv()
            start(remote(theirs, theirs, relay_send.at[at], relay_recv.at[at], core_peer))

    def finish_step(kind, t):
        full = shards[kind][1]
        for way in range(2):
            at = (kind, t - 1, way)
            owner = owner_from(t, way)
            one = part(full, owner * 4 + core_q, t, way)
            remote(one, one, core_send.at[at], core_recv.at[at], core_peer).wait_recv()
            two = part(full, owner * 4 + lax.rem(core_q + 2, 4), t, way)
            remote(two, two, relay_send.at[at], relay_recv.at[at], core_peer).wait_recv()

    def c_part(owner, t, way):
        if t < half:
            return c_all.at[pl.ds(owner * blocks, blocks)]
        return c_all.at[pl.ds(owner * blocks + way * (blocks // 2), blocks // 2)]

    def c_send_step(t, ways=(0, 1)):
        for way in ways:
            piece = c_part(owner_from(t - 1, way), t, way)
            start(remote(
                piece, piece, c_send.at[t - 1, way], c_recv.at[t - 1, way], ring[way]
            ))

    def c_step(t):
        for way in range(2):
            piece = c_part(owner_from(t, way), t, way)
            remote(
                piece, piece, c_send.at[t - 1, way], c_recv.at[t - 1, way], ring[way]
            ).wait_recv()
            if t < half:
                c_send_step(t + 1, (way,))

    coarse_count = blocks * QUART
    fold = BLK // QUART
    to_row = lax.broadcasted_iota(jnp.int32, (coarse_count, own), 0)
    from_row = lax.broadcasted_iota(jnp.int32, (coarse_count, own), 1)
    mean_of = jnp.where(
        (from_row >= to_row * fold) & (from_row < (to_row + 1) * fold), 1.0 / fold, 0.0
    ).astype(jnp.bfloat16)
    means = jnp.dot(mean_of, tok_ref[...], preferred_element_type=jnp.float32)
    c_all[pl.ds(me * blocks, blocks)] = means.astype(jnp.bfloat16).reshape(
        blocks, QUART, tok_ref.shape[1]
    )
    w_all[pl.ds(me * 4, 4)] = w_ref[...]
    wo_all[pl.ds(me * 4, 4)] = wo_ref[...]
    rows_all[pl.ds(BLK, own), :] = tok_ref[...]

    slab_row = lax.broadcasted_iota(jnp.int32, (QUART, listed), 0)
    slab_from = lax.broadcasted_iota(jnp.int32, (QUART, listed), 1)
    for b in range(blocks):
        for i in range(list_len):
            at = (b * list_len + i) * QUART
            level = levels_ref[i, b]
            inside = (slab_from >= at) & (slab_from < at + QUART)
            same = jnp.where(slab_from == slab_row + at, 1.0, 0.0)
            mean = jnp.where(inside, 1.0 / QUART, 0.0)
            pick_all[pl.ds(at, QUART), :] = jnp.where(
                (slab_row == 0) & (level == 2), mean, same
            ).astype(jnp.bfloat16)

    first, last = me == 0, me == n - 1

    @pl.when(first)
    def _():
        rows_all[pl.ds(0, BLK), :] = jnp.zeros((BLK, rows_all.shape[1]), jnp.bfloat16)

    @pl.when(last)
    def _():
        rows_all[pl.ds(BLK + own, BLK), :] = jnp.zeros((BLK, rows_all.shape[1]), jnp.bfloat16)

    pl.semaphore_wait(barrier, 6)

    ring_send_step(0, 1)
    ring_step(0, 1)
    c_send_step(1)
    up = remote(
        tok_ref.at[pl.ds(own - BLK, BLK)], rows_all.at[pl.ds(0, BLK)],
        halo_send.at[0], halo_recv.at[0], after,
    )
    down = remote(
        tok_ref.at[pl.ds(0, BLK)], rows_all.at[pl.ds(BLK + own, BLK)],
        halo_send.at[1], halo_recv.at[1], before,
    )
    pl.when(me < n - 1)(up.start)
    pl.when(me > 0)(down.start)
    for t in range(2, half + 1):
        ring_step(0, t)
        relay_step(0, t - 1)
        if t == 2:
            ring_send_step(1, 1)
        else:
            ring_step(1, t - 2)
            if t > 3:
                relay_step(1, t - 3)
        if t < half:
            c_step(t - 1)
    for t in range(1, half):
        finish_step(0, t)
    relay_step(0, half)
    c_step(half - 1)
    finish_step(0, half)
    pl.when(me > 0)(up.wait_recv)
    pl.when(me < n - 1)(down.wait_recv)

    depth = w_all.shape[0] * w_all.shape[1]
    tile = 256

    def q_tile(j, carry):
        columns = pl.ds(pl.multiple_of(j * tile, tile), tile)
        q_all[:, columns] = jnp.dot(
            rows_all[pl.ds(BLK, own), :], w_all[:, :, columns].reshape(depth, tile),
            preferred_element_type=jnp.float32,
        ).astype(jnp.bfloat16)
        return carry

    def kv_tile(low, count, j, carry):
        columns = pl.ds(pl.multiple_of(j * tile, tile), tile)
        there = pl.ds(pl.multiple_of(width + j * tile, tile), tile)
        kv_all[pl.ds(low, count), columns] = jnp.dot(
            rows_all[pl.ds(low, count), :], w_all[:, :, there].reshape(depth, tile),
            preferred_element_type=jnp.float32,
        ).astype(jnp.bfloat16)
        return carry

    tiles = width // tile
    lax.fori_loop(0, tiles, q_tile, 0)
    lax.fori_loop(0, 2 * tiles, functools.partial(kv_tile, 0, near), 0)
    ring_step(1, half - 1)
    relay_step(1, half - 2)
    c_step(half)

    for b in range(blocks):
        for i in range(list_len):
            at = near + (b * list_len + i) * QUART
            rows_all[pl.ds(at, QUART), :] = c_all[blocks_ref[i, b]]
    lax.fori_loop(0, 2 * tiles, functools.partial(kv_tile, near, listed), 0)
    far_all[...] = jnp.dot(
        pick_all[...], kv_all[pl.ds(near, listed), :], preferred_element_type=jnp.float32
    ).astype(jnp.bfloat16)
    ring_step(1, half)
    relay_step(1, half - 1)

    per = list_len * QUART
    key_count = 3 * BLK + per
    lane = lax.broadcasted_iota(jnp.int32, (1, key_count), 1)
    log2e = math.log2(math.e)

    def attend_block(b):
        bias = jnp.where(lane < 3 * BLK, 0.0, masked_score)
        bias = jnp.where((lane < BLK) & (me * blocks + b == 0), masked_score, bias)
        bias = jnp.where(
            (lane >= 2 * BLK) & (lane < 3 * BLK) & (me * blocks + b == n * blocks - 1),
            masked_score, bias,
        )
        for i in range(list_len):
            level = levels_ref[i, b]
            low = 3 * BLK + i * QUART
            bias = jnp.where(
                (lane >= low) & (lane < low + QUART) & (level == 1),
                math.log2(BLK / QUART), bias,
            )
            bias = jnp.where((lane == low) & (level == 2), math.log2(BLK), bias)
        q_rows = pl.ds(b * BLK, BLK)
        near_rows = pl.ds(b * BLK, 3 * BLK)
        far_rows = pl.ds(b * per, per)
        for low in range(0, HEADS, 6):
            heads = range(low, low + 6)
            scores = []
            for h in heads:
                k_lanes = pl.ds(h * HD, HD)
                keys = jnp.concatenate(
                    [kv_all[near_rows, k_lanes], far_all[far_rows, k_lanes]], 0
                )
                scores.append(lax.dot_general(
                    q_all[q_rows, k_lanes], keys, (((1,), (1,)), ((), ())),
                    preferred_element_type=jnp.float32,
                ))
            scores = [s * (log2e / math.sqrt(HD)) + bias for s in scores]
            tops = [jnp.max(s, axis=-1, keepdims=True) for s in scores]
            exponents = [jnp.exp2(s - top) for s, top in zip(scores, tops)]
            totals = [jnp.sum(e, axis=-1, keepdims=True) for e in exponents]
            weights = [
                (e * (1.0 / total)).astype(jnp.bfloat16) for e, total in zip(exponents, totals)
            ]
            for h, weight in zip(heads, weights):
                v_lanes = pl.ds(width + h * HD, HD)
                values = jnp.concatenate(
                    [kv_all[near_rows, v_lanes], far_all[far_rows, v_lanes]], 0
                )
                att_all[q_rows, pl.ds(h * HD, HD)] = jnp.dot(
                    weight, values, preferred_element_type=jnp.float32
                ).astype(jnp.bfloat16)

    for b in range(blocks):
        attend_block(b)
        if b == 2:
            relay_step(1, half)
    for t in range(1, half + 1):
        finish_step(1, t)

    per_tile = 8
    out_tile = per_tile * wo_all.shape[1]
    for j in range(wo_all.shape[0] // per_tile):
        out_ref[:, pl.ds(j * out_tile, out_tile)] = lax.dot_general(
            att_all[...], wo_all[pl.ds(j * per_tile, per_tile)].reshape(out_tile, width),
            (((1,), (1,)), ((), ())), preferred_element_type=jnp.float32,
        ).astype(jnp.bfloat16)
    pl.when(me < n - 1)(up.wait_send)
    pl.when(me > 0)(down.wait_send)
    for copy in started:
        copy.wait_send()


def per_device_fused(tokens, w_qkv, w_out, key_blocks, key_levels):
    n = lax.axis_size("seq")
    own, model = tokens.shape
    blocks, list_len = key_blocks.shape
    width = HEADS * HD
    half = n // 2
    listed = blocks * list_len * QUART
    near = own + 2 * BLK
    w_rows = w_qkv.shape[0] // 4
    wo_rows = w_out.shape[1] // 4
    bf16 = jnp.bfloat16
    pair = lambda: pltpu.SemaphoreType.DMA((2, half, 2))
    vmem = pl.BlockSpec(memory_space=pltpu.VMEM)
    smem = pl.BlockSpec(memory_space=pltpu.SMEM)
    return pl.pallas_call(
        functools.partial(fused_kernel, n, blocks, list_len),
        out_shape=jax.ShapeDtypeStruct((own, model), bf16),
        in_specs=[smem, smem, vmem, vmem, vmem],
        out_specs=vmem,
        scratch_shapes=[
            pltpu.VMEM((n * 4, w_rows, 3 * width), bf16),
            pltpu.VMEM((n * 4, wo_rows, width), bf16),
            pltpu.VMEM((n * blocks, QUART, model), bf16),
            pltpu.VMEM((near + listed, model), bf16),
            pltpu.VMEM((own, width), bf16),
            pltpu.VMEM((near + listed, 2 * width), bf16),
            pltpu.VMEM((listed, listed), bf16),
            pltpu.VMEM((listed, 2 * width), bf16),
            pltpu.VMEM((own, width), bf16),
            *[pair() for _ in range(8)],
            pltpu.SemaphoreType.DMA((half, 2)),
            pltpu.SemaphoreType.DMA((half, 2)),
            pltpu.SemaphoreType.DMA((2,)),
            pltpu.SemaphoreType.DMA((2,)),
        ],
        compiler_params=pltpu.CompilerParams(
            collective_id=0, has_side_effects=True, vmem_limit_bytes=56 * 1024 * 1024
        ),
    )(
        key_blocks.T, key_levels.T, tokens,
        w_qkv.reshape(4, w_rows, 3 * width), w_out.T.reshape(4, wo_rows, width),
    )


def per_device(tokens, w_qkv, w_out, key_blocks, key_levels):
    blocks, list_len = key_blocks.shape
    fits = (
        lax.axis_size("clip") == 4
        and lax.axis_size("seq") in (4, 6, 8)
        and w_qkv.shape[0] % 64 == 0
        and w_out.shape[1] % 64 == 0
        and blocks % 2 == 0
        and blocks >= 4
        and (3 * BLK + list_len * QUART) % LANES == 0
    )
    form = per_device_fused if fits else per_device_general
    return form(tokens, w_qkv, w_out, key_blocks, key_levels)


def solution(mesh):
    placed = (
        P(("clip", "seq"), None),
        P("seq", None),
        P(None, "seq"),
        P(("clip", "seq"), None),
        P(("clip", "seq"), None),
    )
    return jax.shard_map(
        per_device, mesh=mesh, in_specs=placed, out_specs=P(("clip", "seq"), None), check_vma=False
    )
```

```python
import functools
import math

import jax
import jax.numpy as jnp
from jax import lax
from jax.experimental import pallas as pl
from jax.experimental.pallas import tpu as pltpu
from jax.sharding import PartitionSpec as P

HEADS = 6
HD = 128
BLK = 64
QUART = 16


masked_score = -1e30


def with_halo(block, sides, width):
    for axis, dim in sides:
        count = lax.axis_size(axis)
        forward = [(i, i + 1) for i in range(count - 1)]
        backward = [(target, source) for source, target in forward]
        low = lax.ppermute(
            lax.slice_in_dim(block, block.shape[dim] - width, None, axis=dim), axis, forward
        )
        high = lax.ppermute(lax.slice_in_dim(block, 0, width, axis=dim), axis, backward)
        block = jnp.concatenate([low, block, high], axis=dim)
    return block


def attend(queries, keys_all, score_bias, usable):
    block_count, key_count = (keys_all.shape[0], keys_all.shape[1])
    heads_view = keys_all.reshape(block_count, key_count, 2, HEADS, HD)
    scores = jnp.einsum(
        "bqhd,bkhd->bhqk", queries, heads_view[:, :, 0], preferred_element_type=jnp.float32
    )
    scores = scores * (1.0 / math.sqrt(HD)) + score_bias[:, None, None, :]
    scores = jnp.where(usable[:, None, None, :], scores, masked_score)
    row_top = jnp.max(scores, axis=-1, keepdims=True)
    exponent = jnp.exp(scores - row_top)
    total_mass = jnp.sum(exponent, axis=-1, keepdims=True)
    attn_weights = (exponent / total_mass).astype(jnp.bfloat16)
    attended = jnp.einsum(
        "bhqk,bkhd->bqhd", attn_weights, heads_view[:, :, 1], preferred_element_type=jnp.float32
    )
    return attended.astype(jnp.bfloat16)


def per_device_general(tokens, w_qkv, w_out, key_blocks, key_levels):
    peer_count = lax.axis_size("seq")
    own_index = lax.axis_index("seq")
    tok_rows = tokens.shape[0]
    local_blocks = tok_rows // BLK
    list_len = key_blocks.shape[1]
    slot_count = (local_blocks * list_len + peer_count - 1) // peer_count
    head_width = HEADS * HD
    projected = jnp.dot(
        tokens, lax.all_gather(w_qkv, "seq", axis=0, tiled=True), preferred_element_type=jnp.float32
    ).astype(jnp.bfloat16)
    queries = projected[:, :head_width]
    key_value = projected[:, head_width:]
    kv_blocks = key_value.reshape(local_blocks, BLK, 2 * head_width)
    widened = kv_blocks.astype(jnp.float32).reshape(
        local_blocks, QUART, BLK // QUART, 2 * head_width
    )
    coarse_own = jnp.mean(widened, axis=2).astype(jnp.bfloat16)
    flat_ids = key_blocks.reshape(-1)
    owner_ids = flat_ids // local_blocks
    local_ids = flat_ids % local_blocks
    peer_ids = jnp.arange(peer_count, dtype=jnp.int32)
    slot_ids = jnp.arange(slot_count, dtype=jnp.int32)
    owner_hot = (owner_ids[:, None] == peer_ids[None, :]).astype(jnp.int32)
    slot_rank = jnp.sum((jnp.cumsum(owner_hot, axis=0) - owner_hot) * owner_hot, axis=1)
    slot_hot = (slot_rank[:, None] == slot_ids[None, :]).astype(jnp.int32)
    wanted = jnp.sum(
        owner_hot[:, :, None] * slot_hot[:, None, :] * local_ids[:, None, None], axis=0
    )
    received = lax.all_to_all(
        coarse_own[lax.all_to_all(wanted, "seq", split_axis=0, concat_axis=0, tiled=True)],
        "seq",
        split_axis=0,
        concat_axis=0,
        tiled=True,
    )
    coarse_rows = received[owner_ids, slot_rank]
    single_rows = jnp.mean(coarse_rows.astype(jnp.float32), axis=1).astype(jnp.bfloat16)
    padded = with_halo(kv_blocks, (("seq", 0),), 1)
    near_rows = jnp.concatenate([padded[:-2], padded[1:-1], padded[2:]], axis=1)
    near_ids = (
        own_index * local_blocks
        + jnp.arange(local_blocks, dtype=jnp.int32)[:, None]
        + jnp.arange(3, dtype=jnp.int32)[None, :]
        - 1
    )
    near_ok = (near_ids >= 0) & (near_ids < local_blocks * peer_count)
    keys_all = jnp.concatenate(
        [
            near_rows,
            coarse_rows.reshape(local_blocks, list_len * QUART, 2 * head_width),
            single_rows.reshape(local_blocks, list_len, 2 * head_width),
        ],
        axis=1,
    )
    usable = jnp.concatenate(
        [
            jnp.repeat(near_ok, BLK, axis=1),
            jnp.repeat(key_levels == 1, QUART, axis=1),
            key_levels == 2,
        ],
        axis=1,
    )
    score_bias = jnp.concatenate(
        [
            jnp.zeros((local_blocks, 3 * BLK), jnp.float32),
            jnp.full((local_blocks, list_len * QUART), math.log(BLK / QUART), jnp.float32),
            jnp.full((local_blocks, list_len), math.log(BLK), jnp.float32),
        ],
        axis=1,
    )
    attended = attend(queries.reshape(local_blocks, BLK, HEADS, HD), keys_all, score_bias, usable)
    attended = attended.reshape(tok_rows, head_width)
    return jnp.dot(
        attended,
        lax.all_gather(w_out, "seq", axis=1, tiled=True),
        preferred_element_type=jnp.float32,
    ).astype(jnp.bfloat16)


MESH = pl.DeviceIdType.MESH
LANES = 128


def fused_kernel(
    n, blocks, list_len,
    blocks_ref, levels_ref, tok_ref, w_ref, wo_ref, out_ref,
    w_all, wo_all, c_all, rows_all, q_all, kv_all, pick_all, far_all, att_all,
    ring_send, ring_recv, core_send, core_recv, x_send, x_recv, relay_send, relay_recv,
    c_send, c_recv, halo_send, halo_recv,
):
    me = lax.axis_index("seq")
    clip = lax.axis_index("clip")
    half = n // 2
    own = blocks * BLK
    listed = blocks * list_len * QUART
    near = own + 2 * BLK
    width = HEADS * HD

    def owner_at(pos):
        pos = lax.rem(pos + 2 * n, n)
        return jnp.where(pos < half, 2 * pos, 2 * (n - 1 - pos) + 1)

    pos = jnp.where(lax.rem(me, 2) == 0, me // 2, n - 1 - me // 2)
    ring = ((owner_at(pos + 1), clip), (owner_at(pos - 1), clip))
    core_q = clip + 1 - 2 * lax.rem(clip, 2)
    x_q = lax.rem(clip + 2, 4)
    core_peer, x_peer = (me, core_q), (me, x_q)
    after, before = (lax.rem(me + 1, n), clip), (lax.rem(me + n - 1, n), clip)

    barrier = pltpu.get_barrier_semaphore()
    for peer in (*ring, core_peer, x_peer, after, before):
        pl.semaphore_signal(barrier, inc=1, device_id=peer, device_id_type=MESH)

    def remote(src, dst, send, recv, peer):
        return pltpu.make_async_remote_copy(
            src_ref=src, dst_ref=dst, send_sem=send, recv_sem=recv,
            device_id=peer, device_id_type=MESH,
        )

    started = []

    def start(copy):
        copy.start()
        started.append(copy)

    shards = ((w_ref, w_all), (wo_ref, wo_all))

    def part(ref, slot, t, way):
        lanes = ref.shape[-1]
        if t < half:
            return ref.at[slot]
        return ref.at[slot, :, pl.ds(way * (lanes // 2), lanes // 2)]

    def owner_from(t, way):
        return owner_at(pos - t) if way == 0 else owner_at(pos + t)

    def ring_send_step(kind, t, ways=(0, 1)):
        for way in ways:
            source, full = shards[kind]
            owner = owner_from(t - 1, way)
            slot = owner * 4 + clip
            src = part(source, clip, t, way) if t == 1 else part(full, slot, t, way)
            start(remote(
                src, part(full, slot, t, way),
                ring_send.at[kind, t - 1, way], ring_recv.at[kind, t - 1, way], ring[way],
            ))

    def arrive(kind, t, way):
        full = shards[kind][1]
        mine = part(full, owner_from(t, way) * 4 + clip, t, way)
        remote(
            mine, mine, ring_send.at[kind, t - 1, way], ring_recv.at[kind, t - 1, way], ring[way]
        ).wait_recv()

    def share(kind, t, ways=(0, 1)):
        full = shards[kind][1]
        for way in ways:
            mine = part(full, owner_from(t, way) * 4 + clip, t, way)
            at = (kind, t - 1, way)
            start(remote(mine, mine, x_send.at[at], x_recv.at[at], x_peer))
            start(remote(mine, mine, core_send.at[at], core_recv.at[at], core_peer))

    def ring_step(kind, t):
        for way in range(2):
            arrive(kind, t, way)
            if t < half:
                ring_send_step(kind, t + 1, (way,))
            share(kind, t, (way,))

    def relay_step(kind, t):
        full = shards[kind][1]
        for way in range(2):
            at = (kind, t - 1, way)
            theirs = part(full, owner_from(t, way) * 4 + x_q, t, way)
            remote(theirs, theirs, x_send.at[at], x_recv.at[at], x_peer).wait_recv()
            start(remote(theirs, theirs, relay_send.at[at], relay_recv.at[at], core_peer))

    def finish_step(kind, t):
        full = shards[kind][1]
        for way in range(2):
            at = (kind, t - 1, way)
            owner = owner_from(t, way)
            one = part(full, owner * 4 + core_q, t, way)
            remote(one, one, core_send.at[at], core_recv.at[at], core_peer).wait_recv()
            two = part(full, owner * 4 + lax.rem(core_q + 2, 4), t, way)
            remote(two, two, relay_send.at[at], relay_recv.at[at], core_peer).wait_recv()

    def c_part(owner, t, way):
        if t < half:
            return c_all.at[pl.ds(owner * blocks, blocks)]
        return c_all.at[pl.ds(owner * blocks + way * (blocks // 2), blocks // 2)]

    def c_send_step(t, ways=(0, 1)):
        for way in ways:
            piece = c_part(owner_from(t - 1, way), t, way)
            start(remote(
                piece, piece, c_send.at[t - 1, way], c_recv.at[t - 1, way], ring[way]
            ))

    def c_step(t):
        for way in range(2):
            piece = c_part(owner_from(t, way), t, way)
            remote(
                piece, piece, c_send.at[t - 1, way], c_recv.at[t - 1, way], ring[way]
            ).wait_recv()
            if t < half:
                c_send_step(t + 1, (way,))

    coarse_count = blocks * QUART
    fold = BLK // QUART
    to_row = lax.broadcasted_iota(jnp.int32, (coarse_count, own), 0)
    from_row = lax.broadcasted_iota(jnp.int32, (coarse_count, own), 1)
    mean_of = jnp.where(
        (from_row >= to_row * fold) & (from_row < (to_row + 1) * fold), 1.0 / fold, 0.0
    ).astype(jnp.bfloat16)
    means = jnp.dot(mean_of, tok_ref[...], preferred_element_type=jnp.float32)
    c_all[pl.ds(me * blocks, blocks)] = means.astype(jnp.bfloat16).reshape(
        blocks, QUART, tok_ref.shape[1]
    )
    w_all[pl.ds(me * 4, 4)] = w_ref[...]
    wo_all[pl.ds(me * 4, 4)] = wo_ref[...]
    rows_all[pl.ds(BLK, own), :] = tok_ref[...]

    slab_row = lax.broadcasted_iota(jnp.int32, (QUART, listed), 0)
    slab_from = lax.broadcasted_iota(jnp.int32, (QUART, listed), 1)
    for b in range(blocks):
        for i in range(list_len):
            at = (b * list_len + i) * QUART
            level = levels_ref[i, b]
            inside = (slab_from >= at) & (slab_from < at + QUART)
            same = jnp.where(slab_from == slab_row + at, 1.0, 0.0)
            mean = jnp.where(inside, 1.0 / QUART, 0.0)
            pick_all[pl.ds(at, QUART), :] = jnp.where(
                (slab_row == 0) & (level == 2), mean, same
            ).astype(jnp.bfloat16)

    first, last = me == 0, me == n - 1

    @pl.when(first)
    def _():
        rows_all[pl.ds(0, BLK), :] = jnp.zeros((BLK, rows_all.shape[1]), jnp.bfloat16)

    @pl.when(last)
    def _():
        rows_all[pl.ds(BLK + own, BLK), :] = jnp.zeros((BLK, rows_all.shape[1]), jnp.bfloat16)

    pl.semaphore_wait(barrier, 6)

    ring_send_step(0, 1)
    ring_step(0, 1)
    c_send_step(1)
    up = remote(
        tok_ref.at[pl.ds(own - BLK, BLK)], rows_all.at[pl.ds(0, BLK)],
        halo_send.at[0], halo_recv.at[0], after,
    )
    down = remote(
        tok_ref.at[pl.ds(0, BLK)], rows_all.at[pl.ds(BLK + own, BLK)],
        halo_send.at[1], halo_recv.at[1], before,
    )
    pl.when(me < n - 1)(up.start)
    pl.when(me > 0)(down.start)
    for t in range(2, half + 1):
        ring_step(0, t)
        relay_step(0, t - 1)
        if t == 2:
            ring_send_step(1, 1)
        else:
            ring_step(1, t - 2)
            if t > 3:
                relay_step(1, t - 3)
        if t < half:
            c_step(t - 1)
    for t in range(1, half):
        finish_step(0, t)
    relay_step(0, half)
    c_step(half - 1)
    finish_step(0, half)
    pl.when(me > 0)(up.wait_recv)
    pl.when(me < n - 1)(down.wait_recv)

    depth = w_all.shape[0] * w_all.shape[1]
    tile = 256

    def q_tile(j, carry):
        columns = pl.ds(pl.multiple_of(j * tile, tile), tile)
        q_all[:, columns] = jnp.dot(
            rows_all[pl.ds(BLK, own), :], w_all[:, :, columns].reshape(depth, tile),
            preferred_element_type=jnp.float32,
        ).astype(jnp.bfloat16)
        return carry

    def kv_tile(low, count, j, carry):
        columns = pl.ds(pl.multiple_of(j * tile, tile), tile)
        there = pl.ds(pl.multiple_of(width + j * tile, tile), tile)
        kv_all[pl.ds(low, count), columns] = jnp.dot(
            rows_all[pl.ds(low, count), :], w_all[:, :, there].reshape(depth, tile),
            preferred_element_type=jnp.float32,
        ).astype(jnp.bfloat16)
        return carry

    tiles = width // tile
    lax.fori_loop(0, tiles, q_tile, 0, unroll=True)
    lax.fori_loop(0, 2 * tiles, functools.partial(kv_tile, 0, near), 0, unroll=True)
    ring_step(1, half - 1)
    relay_step(1, half - 2)
    c_step(half)

    for b in range(blocks):
        for i in range(list_len):
            at = near + (b * list_len + i) * QUART
            rows_all[pl.ds(at, QUART), :] = c_all[blocks_ref[i, b]]
    lax.fori_loop(0, 2 * tiles, functools.partial(kv_tile, near, listed), 0, unroll=True)
    far_all[...] = jnp.dot(
        pick_all[...], kv_all[pl.ds(near, listed), :], preferred_element_type=jnp.float32
    ).astype(jnp.bfloat16)
    ring_step(1, half)
    relay_step(1, half - 1)

    per = list_len * QUART
    key_count = 3 * BLK + per
    lane = lax.broadcasted_iota(jnp.int32, (1, key_count), 1)
    log2e = math.log2(math.e)

    def attend_block(b):
        bias = jnp.where(lane < 3 * BLK, 0.0, masked_score)
        bias = jnp.where((lane < BLK) & (me * blocks + b == 0), masked_score, bias)
        bias = jnp.where(
            (lane >= 2 * BLK) & (lane < 3 * BLK) & (me * blocks + b == n * blocks - 1),
            masked_score, bias,
        )
        for i in range(list_len):
            level = levels_ref[i, b]
            low = 3 * BLK + i * QUART
            bias = jnp.where(
                (lane >= low) & (lane < low + QUART) & (level == 1),
                math.log2(BLK / QUART), bias,
            )
            bias = jnp.where((lane == low) & (level == 2), math.log2(BLK), bias)
        q_rows = pl.ds(b * BLK, BLK)
        near_rows = pl.ds(b * BLK, 3 * BLK)
        far_rows = pl.ds(b * per, per)
        for low in range(0, HEADS, 6):
            heads = range(low, low + 6)
            scores = []
            for h in heads:
                k_lanes = pl.ds(h * HD, HD)
                keys = jnp.concatenate(
                    [kv_all[near_rows, k_lanes], far_all[far_rows, k_lanes]], 0
                )
                scores.append(lax.dot_general(
                    q_all[q_rows, k_lanes], keys, (((1,), (1,)), ((), ())),
                    preferred_element_type=jnp.float32,
                ))
            scores = [s * (log2e / math.sqrt(HD)) + bias for s in scores]
            tops = [jnp.max(s, axis=-1, keepdims=True) for s in scores]
            exponents = [jnp.exp2(s - top) for s, top in zip(scores, tops)]
            totals = [jnp.sum(e, axis=-1, keepdims=True) for e in exponents]
            weights = [
                (e * (1.0 / total)).astype(jnp.bfloat16) for e, total in zip(exponents, totals)
            ]
            def combine():
                for h, weight in zip(heads, weights):
                    v_lanes = pl.ds(width + h * HD, HD)
                    values = jnp.concatenate(
                        [kv_all[near_rows, v_lanes], far_all[far_rows, v_lanes]], 0
                    )
                    att_all[q_rows, pl.ds(h * HD, HD)] = jnp.dot(
                        weight, values, preferred_element_type=jnp.float32
                    ).astype(jnp.bfloat16)
            return combine

    combine = None
    for b in range(blocks):
        ahead = attend_block(b)
        if combine is not None:
            combine()
        combine = ahead
        if b == 2:
            relay_step(1, half)
    combine()
    for t in range(1, half + 1):
        finish_step(1, t)

    per_tile = 8
    out_tile = per_tile * wo_all.shape[1]
    for j in range(wo_all.shape[0] // per_tile):
        out_ref[:, pl.ds(j * out_tile, out_tile)] = lax.dot_general(
            att_all[...], wo_all[pl.ds(j * per_tile, per_tile)].reshape(out_tile, width),
            (((1,), (1,)), ((), ())), preferred_element_type=jnp.float32,
        ).astype(jnp.bfloat16)
    pl.when(me < n - 1)(up.wait_send)
    pl.when(me > 0)(down.wait_send)
    for copy in started:
        copy.wait_send()


def per_device_fused(tokens, w_qkv, w_out, key_blocks, key_levels):
    n = lax.axis_size("seq")
    own, model = tokens.shape
    blocks, list_len = key_blocks.shape
    width = HEADS * HD
    half = n // 2
    listed = blocks * list_len * QUART
    near = own + 2 * BLK
    w_rows = w_qkv.shape[0] // 4
    wo_rows = w_out.shape[1] // 4
    bf16 = jnp.bfloat16
    pair = lambda: pltpu.SemaphoreType.DMA((2, half, 2))
    vmem = pl.BlockSpec(memory_space=pltpu.VMEM)
    smem = pl.BlockSpec(memory_space=pltpu.SMEM)
    return pl.pallas_call(
        functools.partial(fused_kernel, n, blocks, list_len),
        out_shape=jax.ShapeDtypeStruct((own, model), bf16),
        in_specs=[smem, smem, vmem, vmem, vmem],
        out_specs=vmem,
        scratch_shapes=[
            pltpu.VMEM((n * 4, w_rows, 3 * width), bf16),
            pltpu.VMEM((n * 4, wo_rows, width), bf16),
            pltpu.VMEM((n * blocks, QUART, model), bf16),
            pltpu.VMEM((near + listed, model), bf16),
            pltpu.VMEM((own, width), bf16),
            pltpu.VMEM((near + listed, 2 * width), bf16),
            pltpu.VMEM((listed, listed), bf16),
            pltpu.VMEM((listed, 2 * width), bf16),
            pltpu.VMEM((own, width), bf16),
            *[pair() for _ in range(8)],
            pltpu.SemaphoreType.DMA((half, 2)),
            pltpu.SemaphoreType.DMA((half, 2)),
            pltpu.SemaphoreType.DMA((2,)),
            pltpu.SemaphoreType.DMA((2,)),
        ],
        compiler_params=pltpu.CompilerParams(
            collective_id=0, has_side_effects=True, vmem_limit_bytes=56 * 1024 * 1024
        ),
    )(
        key_blocks.T, key_levels.T, tokens,
        w_qkv.reshape(4, w_rows, 3 * width), w_out.T.reshape(4, wo_rows, width),
    )


def per_device(tokens, w_qkv, w_out, key_blocks, key_levels):
    blocks, list_len = key_blocks.shape
    fits = (
        lax.axis_size("clip") == 4
        and lax.axis_size("seq") in (4, 6, 8)
        and w_qkv.shape[0] % 64 == 0
        and w_out.shape[1] % 64 == 0
        and blocks % 2 == 0
        and blocks >= 4
        and (3 * BLK + list_len * QUART) % LANES == 0
    )
    form = per_device_fused if fits else per_device_general
    return form(tokens, w_qkv, w_out, key_blocks, key_levels)


def solution(mesh):
    placed = (
        P(("clip", "seq"), None),
        P("seq", None),
        P(None, "seq"),
        P(("clip", "seq"), None),
        P(("clip", "seq"), None),
    )
    return jax.shard_map(
        per_device, mesh=mesh, in_specs=placed, out_specs=P(("clip", "seq"), None), check_vma=False
    )
```
